128 devices in a mesh: basis: 16 (over z, y_hi, core), aux: 8 (over x, y_lo).
Axes of the slice: x: 4, y: 4 (y_hi: 2, y_lo: 2; y = y_hi * 2 + y_lo), z: 4, core: 2. Of those that a mesh axis runs over, the one named last changes fastest.
Arguments:
- three_index: bfloat16 [1536, 16, 8192], P('aux', None, 'basis'), may hold values from -0.47851562 to 0.47851562
Outputs:
- exchange: float32 [8192, 8192], P(('basis', 'aux'))
The draws below stay inside these ranges and needn't reach their ends.
All inputs are finite; a program needn't handle non-finite values.
Results may differ from the reference program's by a relative error of at most 0.0003.
Values may be sent and summed in bfloat16 or wider, within the bound.
A program may use at most 192 MiB of HBM per device.

```python
import jax
import jax.numpy as jnp

NOCC = 16
NBASIS = 8192
NAUX = 1536


def level_of(key, shape, split, smallest, top_value):
    factor_of = 1.0
    for position, parts in split:
        draws = jax.random.uniform(jax.random.fold_in(jax.random.fold_in(key, 6), position), (parts,), jnp.float32, smallest / len(split), top_value / len(split))
        factor_of = factor_of * jnp.repeat(jnp.exp(draws), shape[position] // parts).reshape((-1,) + (1,) * (len(shape) - 1 - position))
    return factor_of


def scatter_about(rng, shape, spread, limit, cuts=(), held_as=jnp.bfloat16):
    drawn = spread * jax.random.normal(rng, shape, jnp.float32)
    if cuts:
        drawn = drawn * level_of(rng, shape, cuts, -0.22, 0.18)
    return jnp.clip(drawn, -limit, limit).astype(held_as)


def setup_inputs(seed: int = 0) -> dict:
    streams_of = jax.random.split(jax.random.key(seed), 2)
    three_index = scatter_about(streams_of[0], (NAUX, NOCC, NBASIS), ((NAUX * NOCC) ** -0.25), 0.47851562, ((0, 8), (2, 16)))
    return dict(three_index=three_index)


def reference(three_index):
    fitted_rows = three_index.reshape(three_index.shape[0] * three_index.shape[1], three_index.shape[2])
    return jnp.dot(fitted_rows.T, fitted_rows, preferred_element_type=jnp.float32)
```

```python
import jax
import jax.numpy as jnp
from jax import lax
from jax.experimental import pallas as pl
from jax.experimental.pallas import tpu as pltpu
from jax.sharding import PartitionSpec as P

MESH = pl.DeviceIdType.MESH


def position():
    b = lax.axis_index("basis")
    a = lax.axis_index("aux")
    return b // 4, (b // 2) % 2, b % 2, a // 2, a % 2


def device(z, h, c, x, l):
    return (z * 4 + h * 2 + c, x * 2 + l)


def greet(senders, count):
    barrier = pltpu.get_barrier_semaphore()
    for who in senders:
        pl.semaphore_signal(barrier, inc=1, device_id=who, device_id_type=MESH)
    pl.semaphore_wait(barrier, count)


def remote(src, dst, send, recv, who):
    return pltpu.make_async_remote_copy(
        src_ref=src, dst_ref=dst, send_sem=send, recv_sem=recv,
        device_id=who, device_id_type=MESH,
    )


def products(a_ref, f_ref, rows, cols, part, got1, got2, ls, ss, rs, s1, r1, s2, r2):
    z, h, c, x, l = position()
    m = 1 - l
    mate = device(z, h, c, x, m)
    other = device(z, 1 - h, c, x, m)
    core = device(z, h, 1 - c, x, l)
    down = device((z + 3) % 4, h, c, x, l)
    up = device((z + 1) % 4, h, c, x, l)
    far = device((z + 2) % 4, h, c, x, l)
    xa = x + 1 - 2 * (x % 2)
    xb = 3 - x
    xo = 3 - xa
    near_a = device(z, h, c, xa, l)
    near_b = device(z, h, c, xb, l)
    greet([mate, other, core, up, far, near_a, near_b], 7)

    half = rows.shape[3]

    def own(g):
        return a_ref.at[:, pl.ds(pl.multiple_of(g * half, half), half)]

    def copy(n, src, dst, who):
        return remote(src, dst, ss.at[n], rs.at[n], who)

    mate1 = copy(0, own(m), rows.at[1, m], mate)
    other1 = copy(1, own(1), rows.at[3, 1], other)
    down1 = copy(2, own(l), cols.at[2 + l, 0], down)
    core1 = copy(3, own(l), cols.at[l, 1], core)
    mate2 = copy(4, own(l), rows.at[1, l], mate)
    other2 = copy(5, own(0), rows.at[3, 0], other)
    down2 = copy(6, rows.at[1, l], cols.at[2 + m, 0], down)
    core2 = copy(7, rows.at[1, l], cols.at[m, 1], core)
    take = ((z + 2) % 4) // 2
    far1 = copy(8, rows.at[(take + l) % 2, l], cols.at[4, 0], far)
    core3 = copy(9, cols.at[2 + l, 0], cols.at[2 + l, 1], core)
    core4 = copy(10, cols.at[2 + m, 0], cols.at[2 + m, 1], core)
    core5 = copy(11, cols.at[4, 0], cols.at[4, 1], core)
    relay1 = copy(12, rows.at[1, 0], rows.at[2, 0], other)
    relay2 = copy(13, rows.at[3, 1], rows.at[2, 1], mate)

    mate1.start()
    other1.start()
    down1.start()
    core1.start()
    load0 = pltpu.make_async_copy(own(0), rows.at[0, 0], ls.at[0])
    load1 = pltpu.make_async_copy(own(1), rows.at[0, 1], ls.at[1])
    load2 = pltpu.make_async_copy(own(l), cols.at[l, 0], ls.at[2])
    load0.start()
    load1.start()
    load2.start()

    def multiply(i, hr, role, column, first):
        def body(n, carry):
            g = n // 2
            cr = n % 2
            block = lax.dot_general(
                rows[role, g], cols[column, cr], (((0,), (0,)), ((), ())),
                preferred_element_type=jnp.float32,
            ).reshape(2, 128, half)
            if first:
                part[i, hr, cr, pl.ds(2 * g, 2)] = block
            else:
                part[i, hr, cr, pl.ds(2 * g, 2)] += block
            return carry

        lax.fori_loop(0, 4, body, 0)

    def scatter1(i, hr):
        n = i * 2 + hr
        out = []
        for cr, near, mine, kept in ((0, near_a, xa, xo), (1, near_b, xb, xo)):
            for k, piece in ((0, mine), (1, kept)):
                out.append(remote(
                    part.at[i, hr, cr, piece], got1.at[n, cr, k],
                    s1.at[n, cr, k], r1.at[n, cr, k], near,
                ))
        return out

    def scatter2(i, hr):
        n = i * 2 + hr
        out = []
        for cr, near, piece in ((0, near_b, xb), (1, near_a, xa)):
            out.append(remote(
                part.at[i, hr, cr, piece], got2.at[n, cr], s2.at[n, cr], r2.at[n, cr], near,
            ))
        return out

    def begin(i, hr):
        for one in scatter1(i, hr):
            one.start()

    def middle(i, hr):
        n = i * 2 + hr
        for one in scatter1(i, hr):
            one.wait_recv()
        part[i, hr, 0, xb] += got1[n, 0, 1]
        part[i, hr, 1, xa] += got1[n, 1, 1]
        for one in scatter2(i, hr):
            one.start()

    def finish(i, hr):
        n = i * 2 + hr
        for one in scatter2(i, hr):
            one.wait_recv()
        for cr in range(2):
            f_ref[i, hr, cr] = part[i, hr, cr, x] + got1[n, cr, 0] + got2[n, cr]

    load0.wait()
    load1.wait()
    load2.wait()
    core1.wait_recv()
    multiply(0, 0, 0, l, True)

    mate1.wait_recv()
    down2.start()
    core2.start()
    load3 = pltpu.make_async_copy(rows.at[1, l], cols.at[m, 0], ls.at[3])
    load3.start()
    mate1.wait_send()
    mate2.start()
    other1.wait_send()
    other2.start()
    down1.wait_recv()
    core3.start()
    core3.wait_recv()
    multiply(1, 0, 0, 2 + l, True)

    other1.wait_recv()
    mate2.wait_recv()
    other2.wait_recv()
    relay1.start()
    relay2.start()
    load3.wait()
    core2.wait_recv()
    multiply(0, 0, 1, m, False)
    begin(0, 0)
    down2.wait_recv()
    core4.start()
    far1.start()
    core4.wait_recv()
    multiply(1, 0, 1, 2 + m, False)
    begin(1, 0)
    multiply(0, 1, 3, m, True)
    multiply(1, 1, 3, 2 + m, True)
    middle(0, 0)
    middle(1, 0)
    far1.wait_recv()
    core5.start()
    core5.wait_recv()
    late = (z // 2 + l) % 2
    multiply(2, 0, late, 4, True)
    begin(2, 0)
    relay1.wait_recv()
    relay2.wait_recv()
    multiply(0, 1, 2, l, False)
    begin(0, 1)
    multiply(1, 1, 2, 2 + l, False)
    begin(1, 1)
    multiply(2, 1, 2 + late, 4, True)
    begin(2, 1)
    finish(0, 0)
    finish(1, 0)
    middle(2, 0)
    middle(0, 1)
    middle(1, 1)
    middle(2, 1)
    for i, hr in ((2, 0), (0, 1), (1, 1), (2, 1)):
        finish(i, hr)
    for one in (other1, down1, core1, mate1, mate2, other2, down2, core2, far1, core3, core4,
                core5, relay1, relay2):
        if one is not mate1 and one is not other1:
            one.wait_send()
    for i in range(3):
        for hr in range(2):
            for one in scatter1(i, hr) + scatter2(i, hr):
                one.wait_send()


def exchange(f_ref, out_ref, turned, byrow, bycol, ss, rs, st, rt):
    z, h, c, x, l = position()
    m = 1 - l
    mate = device(z, h, c, x, m)
    far = device(z, 1 - h, c, x, l)
    other = device(z, 1 - h, c, x, m)
    senders = [mate, far, other]
    for i in (1, 2):
        for cs in range(2):
            for xs in range(4):
                senders.append(device((z + 4 - i) % 4, h, cs, xs, x // 2))
    greet(senders, 19)

    rowwise = []
    for role, hr, lr, who in ((1, 0, m, mate), (2, 1, l, far), (3, 1, m, other)):
        rowwise.append(remote(
            f_ref.at[:, hr, :, pl.ds(pl.multiple_of(lr * 64, 64), 64), :], byrow.at[role],
            ss.at[role], rs.at[role], who,
        ))
    for one in rowwise:
        one.start()
    colwise = []
    for i in (2, 1):
        for cr in range(2):
            for hr in range(2):
                turned[i - 1, cr, hr] = f_ref[i, hr, cr].T
            for xs in range(2):
                for lr in range(2):
                    one = remote(
                        turned.at[i - 1, cr, :, pl.ds(xs * 128 + lr * 64, 64), :],
                        bycol.at[i - 1, c, x],
                        st.at[i - 1, cr, xs, lr], rt.at[i - 1, c, x],
                        device((z + i) % 4, h, (c + cr) % 2, 2 * l + xs, lr),
                    )
                    one.start()
                    colwise.append(one)
    byrow[0] = f_ref[:, 0, :, pl.ds(pl.multiple_of(l * 64, 64), 64), :]

    def place(zs, hs, cs, at, width):
        return pl.ds(pl.multiple_of(zs * 2048 + hs * 1024 + cs * 512 + at, width), width)

    for i in (1, 2):
        for cs in range(2):
            for xs in range(4):
                remote(
                    turned.at[i - 1, 0, :, pl.ds(0, 64), :], bycol.at[i - 1, cs, xs],
                    st.at[i - 1, 0, 0, 0], rt.at[i - 1, cs, xs], mate,
                ).wait_recv()
                for hr in range(2):
                    out_ref[:, place((z + 4 - i) % 4, (h + hr) % 2, cs, xs * 128, 128)] = bycol[i - 1, cs, xs, hr]
    for one in rowwise:
        one.wait_recv()
    for role, hr, lr in ((0, 0, l), (1, 0, m), (2, 1, l), (3, 1, m)):
        for i in range(3):
            for cr in range(2):
                where = place((z + i) % 4, (h + hr) % 2, (c + cr) % 2, lr * 256, 256)
                if i == 2:
                    out_ref[:, where] += byrow[role, i, cr]
                else:
                    out_ref[:, where] = byrow[role, i, cr]
    for one in rowwise + colwise:
        one.wait_send()


def shards(three_index):
    depth = three_index.shape[0] * three_index.shape[1]
    own = three_index.reshape(depth, 512)
    dma = pltpu.SemaphoreType.DMA
    sums = pl.pallas_call(
        products,
        out_shape=jax.ShapeDtypeStruct((3, 2, 2, 128, 256), jnp.float32),
        in_specs=[pl.BlockSpec(memory_space=pl.ANY)],
        out_specs=pl.BlockSpec(memory_space=pltpu.VMEM),
        scratch_shapes=[
            pltpu.VMEM((4, 2, depth, 256), jnp.bfloat16),
            pltpu.VMEM((5, 2, depth, 256), jnp.bfloat16),
            pltpu.VMEM((3, 2, 2, 4, 128, 256), jnp.float32),
            pltpu.VMEM((6, 2, 2, 128, 256), jnp.float32),
            pltpu.VMEM((6, 2, 128, 256), jnp.float32),
            dma((4,)), dma((14,)), dma((14,)),
            dma((6, 2, 2)), dma((6, 2, 2)), dma((6, 2)), dma((6, 2)),
        ],
        compiler_params=pltpu.CompilerParams(
            collective_id=0, has_side_effects=True, vmem_limit_bytes=56 * 2**20
        ),
        cost_estimate=pl.CostEstimate(flops=16 * 10**9, bytes_accessed=8 * 10**6, transcendentals=0),
    )(own)
    return pl.pallas_call(
        exchange,
        out_shape=jax.ShapeDtypeStruct((64, 8192), jnp.float32),
        in_specs=[pl.BlockSpec(memory_space=pltpu.VMEM)],
        out_specs=pl.BlockSpec(memory_space=pltpu.VMEM),
        scratch_shapes=[
            pltpu.VMEM((2, 2, 2, 256, 128), jnp.float32),
            pltpu.VMEM((4, 3, 2, 64, 256), jnp.float32),
            pltpu.VMEM((2, 2, 4, 2, 64, 128), jnp.float32),
            dma((4,)), dma((4,)), dma((2, 2, 2, 2)), dma((2, 2, 4)),
        ],
        compiler_params=pltpu.CompilerParams(
            collective_id=1, has_side_effects=True, vmem_limit_bytes=32 * 2**20
        ),
    )(sums)


def solution(mesh):
    return jax.shard_map(
        shards,
        mesh=mesh,
        in_specs=(P("aux", None, "basis"),),
        out_specs=P(("basis", "aux"), None),
        check_vma=False,
    )
```

```python
import jax
import jax.numpy as jnp
from jax import lax
from jax.experimental import pallas as pl
from jax.experimental.pallas import tpu as pltpu
from jax.sharding import PartitionSpec as P

MESH = pl.DeviceIdType.MESH


def position():
    b = lax.axis_index("basis")
    a = lax.axis_index("aux")
    return b // 4, (b // 2) % 2, b % 2, a // 2, a % 2


def device(z, h, c, x, l):
    return (z * 4 + h * 2 + c, x * 2 + l)


def remote(src, dst, send, recv, who):
    return pltpu.make_async_remote_copy(
        src_ref=src, dst_ref=dst, send_sem=send, recv_sem=recv,
        device_id=who, device_id_type=MESH,
    )


def kernel(a_ref, out_ref, stage, rows, cols, part, got1, got2, done, turned, byrow, bycol,
           ls, ss, rs, s1, r1, s2, r2, sr, rr, st, rt):
    z, h, c, x, l = position()
    m = 1 - l
    mate = device(z, h, c, x, m)
    other = device(z, 1 - h, c, x, m)
    cross = device(z, 1 - h, c, x, l)
    core = device(z, h, 1 - c, x, l)
    down = device((z + 3) % 4, h, c, x, l)
    up = device((z + 1) % 4, h, c, x, l)
    far = device((z + 2) % 4, h, c, x, l)
    xa = x + 1 - 2 * (x % 2)
    xb = 3 - x
    xo = 3 - xa
    near_a = device(z, h, c, xa, l)
    near_b = device(z, h, c, xb, l)
    depth = a_ref.shape[0]
    half = rows.shape[3]
    quarter = depth // 4

    barrier = pltpu.get_barrier_semaphore()
    senders = [mate, other, cross, core, up, near_a, near_b]
    for i in (1, 2):
        for cs in range(2):
            for xs in range(4):
                senders.append(device((z + 4 - i) % 4, h, cs, xs, l))
    for who in senders:
        pl.semaphore_signal(barrier, inc=1, device_id=who, device_id_type=MESH)

    loads = [
        pltpu.make_async_copy(
            a_ref.at[pl.ds(q * quarter, quarter)], stage.at[pl.ds(q * quarter, quarter)], ls.at[q]
        )
        for q in range(4)
    ]
    for one in loads:
        one.start()
    for q in range(4):
        loads[q].wait()

        def sort(n, carry):
            at = pl.multiple_of(q * quarter + n * 128, 128)
            block = stage[pl.ds(at, 128), :]
            for g in range(2):
                rows[0, g, pl.ds(at, 128), :] = jnp.concatenate(
                    [block[:, t * 128 + g * 64 : t * 128 + g * 64 + 64] for t in range(4)], axis=1
                )
            return carry

        lax.fori_loop(0, quarter // 128, sort, 0)
    pl.semaphore_wait(barrier, len(senders))

    def copy(n, src, dst, who):
        return remote(src, dst, ss.at[n], rs.at[n], who)

    mate1 = copy(0, rows.at[0, m], rows.at[1, m], mate)
    mate2 = copy(1, rows.at[0, l], rows.at[1, l], mate)
    relay2 = copy(2, rows.at[3, m], rows.at[2, m], mate)
    other1 = copy(3, rows.at[0, l], rows.at[3, l], other)
    relay1 = copy(4, rows.at[1, l], rows.at[2, l], other)
    other2 = copy(5, rows.at[0, m], rows.at[3, m], other)
    down1 = copy(6, rows.at[0, l], cols.at[2 + l, 0], down)
    down2 = copy(7, rows.at[1, l], cols.at[2 + m, 0], down)
    take = ((z + 2) % 4) // 2
    far1 = copy(8, rows.at[(take + l) % 2, l], cols.at[4, 0], far)
    core1 = copy(9, rows.at[0, l], cols.at[l, 1], core)
    core2 = copy(10, rows.at[1, l], cols.at[m, 1], core)
    core3 = copy(11, cols.at[2 + l, 0], cols.at[2 + l, 1], core)
    core4 = copy(12, cols.at[2 + m, 0], cols.at[2 + m, 1], core)
    core5 = copy(13, cols.at[4, 0], cols.at[4, 1], core)
    keep1 = pltpu.make_async_copy(rows.at[0, l], cols.at[l, 0], ls.at[4])
    keep2 = pltpu.make_async_copy(rows.at[1, l], cols.at[m, 0], ls.at[5])

    def multiply(i, hr, role, g, column, first):
        def body(cr, carry):
            block = lax.dot_general(
                rows[role, g], cols[column, cr], (((0,), (0,)), ((), ())),
                preferred_element_type=jnp.float32,
            ).reshape(4, 64, half)
            if first:
                part[i, hr, g, cr] = block
            else:
                part[i, hr, g, cr] += block
            return carry

        lax.fori_loop(0, 2, body, 0)

    def scatter1(i, hr, g):
        return [
            remote(
                part.at[i, hr, g, cr, piece], got1.at[i, hr, g, cr, k],
                s1.at[i, hr, g, cr, k], r1.at[i, hr, g, cr, k], near,
            )
            for cr, near, mine in ((0, near_a, xa), (1, near_b, xb))
            for k, piece in ((0, mine), (1, xo))
        ]

    def scatter2(i, hr, g):
        return [
            remote(
                part.at[i, hr, g, cr, piece], got2.at[i, hr, g, cr],
                s2.at[i, hr, g, cr], r2.at[i, hr, g, cr], near,
            )
            for cr, near, piece in ((0, near_b, xb), (1, near_a, xa))
        ]

    def begin(i, hr, g):
        for one in scatter1(i, hr, g):
            one.start()

    def middle(i, hr, g):
        for one in scatter1(i, hr, g):
            one.wait_recv()
        part[i, hr, g, 0, xb] += got1[i, hr, g, 0, 1]
        part[i, hr, g, 1, xa] += got1[i, hr, g, 1, 1]
        for one in scatter2(i, hr, g):
            one.start()

    def finish(i, hr, g):
        for one in scatter2(i, hr, g):
            one.wait_recv()
        for cr in range(2):
            done[i, hr, cr, pl.ds(pl.multiple_of(g * 64, 64), 64), :] = (
                part[i, hr, g, cr, x] + got1[i, hr, g, cr, 0] + got2[i, hr, g, cr]
            )

    def rowwise(i, hr, g, who):
        return remote(
            done.at[i, hr, :, pl.ds(pl.multiple_of(g * 64, 64), 64), :], byrow.at[hr, l, i],
            sr.at[i, hr, g], rr.at[i, hr, l], who,
        )

    def colwise(i, hr):
        return [
            remote(
                turned.at[i - 1, hr, cr, pl.ds(xs * 64, 64)], bycol.at[i - 1, hr, c, x],
                st.at[i - 1, hr, cr, xs], rt.at[i - 1, hr, c, x],
                device((z + i) % 4, h, (c + cr) % 2, xs, l),
            )
            for cr in range(2)
            for xs in range(4)
        ]

    def turn(i, hr):
        for cr in range(2):
            turned[i - 1, hr, cr] = done[i, hr, cr].T
        for one in colwise(i, hr):
            one.start()

    late = (z // 2 + l) % 2

    mate1.start()
    other1.start()
    down1.start()
    core1.start()
    keep1.start()

    @pl.when(take == l)
    def _():
        far1.start()

    keep1.wait()
    core1.wait_recv()
    multiply(0, 0, 0, l, l, True)
    multiply(0, 0, 0, m, l, True)

    mate1.wait_recv()
    down2.start()
    core2.start()
    keep2.start()
    mate1.wait_send()
    mate2.start()
    other1.wait_send()
    relay1.start()

    @pl.when(take != l)
    def _():
        far1.start()

    keep2.wait()
    core2.wait_recv()
    multiply(0, 0, 1, l, m, False)
    begin(0, 0, l)
    other1.wait_recv()
    multiply(0, 1, 3, m, m, True)
    down1.wait_recv()
    core3.start()
    core3.wait_recv()
    multiply(1, 0, 0, l, 2 + l, True)
    multiply(1, 0, 0, m, 2 + l, True)
    middle(0, 0, l)

    mate2.wait_send()
    relay2.start()
    relay1.wait_send()
    other2.start()
    mate2.wait_recv()
    multiply(0, 0, 1, m, m, False)
    begin(0, 0, m)
    relay1.wait_recv()
    multiply(0, 1, 2, m, l, False)
    begin(0, 1, m)
    multiply(1, 1, 2, m, 2 + l, True)
    finish(0, 0, l)
    middle(0, 0, m)
    middle(0, 1, m)
    down2.wait_recv()
    core4.start()
    core4.wait_recv()
    multiply(1, 0, 1, l, 2 + m, False)
    begin(1, 0, l)
    multiply(1, 0, 1, m, 2 + m, False)
    begin(1, 0, m)
    multiply(1, 1, 3, m, 2 + m, False)
    begin(1, 1, m)
    finish(0, 0, m)
    finish(0, 1, m)
    middle(1, 0, l)
    far1.wait_recv()
    core5.start()
    middle(1, 0, m)
    core5.wait_recv()
    multiply(2, 0, late, l, 4, True)
    begin(2, 0, l)
    multiply(2, 0, late, m, 4, True)
    begin(2, 0, m)
    multiply(2, 1, 2 + late, m, 4, True)
    begin(2, 1, m)
    middle(1, 1, m)
    finish(1, 0, l)
    finish(1, 0, m)
    turn(1, 0)

    other2.wait_recv()
    relay2.wait_recv()
    multiply(1, 1, 3, l, 2 + m, True)
    multiply(1, 1, 2, l, 2 + l, False)
    begin(1, 1, l)
    rowwise(0, 0, m, mate).start()
    rowwise(0, 1, m, other).start()
    rowwise(1, 0, m, mate).start()
    multiply(2, 1, 2 + late, l, 4, True)
    begin(2, 1, l)
    multiply(0, 1, 3, l, m, True)
    multiply(0, 1, 2, l, l, False)
    begin(0, 1, l)
    middle(2, 0, l)
    middle(2, 0, m)
    middle(2, 1, m)
    middle(1, 1, l)
    finish(1, 1, m)
    rowwise(1, 1, m, other).start()
    middle(2, 1, l)
    middle(0, 1, l)
    finish(2, 0, l)
    finish(2, 0, m)
    rowwise(2, 0, m, mate).start()
    turn(2, 0)
    finish(2, 1, m)
    rowwise(2, 1, m, other).start()
    finish(1, 1, l)
    rowwise(1, 1, l, cross).start()
    turn(1, 1)
    finish(2, 1, l)
    rowwise(2, 1, l, cross).start()
    turn(2, 1)
    finish(0, 1, l)
    rowwise(0, 1, l, cross).start()

    def place(zs, hs, cs, at):
        return pl.ds(pl.multiple_of(zs * 2048 + hs * 1024 + cs * 512 + at, 128), 128)

    for hr in range(2):
        for i in (1, 2):
            for cs in range(2):
                for xs in range(4):
                    remote(
                        turned.at[i - 1, hr, 0, pl.ds(0, 64)], bycol.at[i - 1, hr, cs, xs],
                        st.at[i - 1, hr, 0, 0], rt.at[i - 1, hr, cs, xs], mate,
                    ).wait_recv()
                    out_ref[:, place((z + 4 - i) % 4, (h + hr) % 2, cs, xs * 128)] = bycol[i - 1, hr, cs, xs]
    for i in range(3):
        for cr in range(2):
            byrow[0, l, i, cr] = done[i, 0, cr, pl.ds(pl.multiple_of(l * 64, 64), 64), :]
    low = lax.broadcasted_iota(jnp.int32, (64, 128), 1) < 64
    for hr in range(2):
        for i in range(3):
            if hr == 0:
                rowwise(i, 0, m, mate).wait_send()
                remote(byrow.at[0, m, i], byrow.at[0, m, i], sr.at[i, 0, m], rr.at[i, 0, m], mate).wait_recv()
            else:
                for g in range(2):
                    remote(byrow.at[1, g, i], byrow.at[1, g, i], sr.at[i, 1, g], rr.at[i, 1, g], mate).wait_recv()
            for cr in range(2):
                for t in range(2):
                    v0 = byrow[hr, 0, i, cr, :, t * 128 : t * 128 + 128]
                    v1 = byrow[hr, 1, i, cr, :, t * 128 : t * 128 + 128]
                    even = jnp.where(low, v0, pltpu.roll(v1, 64, 1))
                    odd = jnp.where(low, pltpu.roll(v0, 64, 1), v1)
                    for value, xs in ((even, 2 * t), (odd, 2 * t + 1)):
                        where = place((z + i) % 4, (h + hr) % 2, (c + cr) % 2, xs * 128)
                        if i == 2:
                            out_ref[:, where] += value
                        else:
                            out_ref[:, where] = value

    for one in (mate2, relay2, relay1, other2, down1, down2, far1, core1, core2, core3, core4, core5):
        if one is not mate2 and one is not relay1:
            one.wait_send()
    for i in range(3):
        for hr in range(2):
            for g in range(2):
                for one in scatter1(i, hr, g) + scatter2(i, hr, g):
                    one.wait_send()
                if hr == 1:
                    rowwise(i, 1, g, cross).wait_send()
            if i:
                for one in colwise(i, hr):
                    one.wait_send()


def shards(three_index):
    depth = three_index.shape[0] * three_index.shape[1]
    own = three_index.reshape(depth, 512)
    dma = pltpu.SemaphoreType.DMA
    f32 = jnp.float32
    return pl.pallas_call(
        kernel,
        out_shape=jax.ShapeDtypeStruct((64, 8192), f32),
        in_specs=[pl.BlockSpec(memory_space=pl.ANY)],
        out_specs=pl.BlockSpec(memory_space=pltpu.VMEM),
        scratch_shapes=[
            pltpu.VMEM((depth, 512), jnp.bfloat16),
            pltpu.VMEM((4, 2, depth, 256), jnp.bfloat16),
            pltpu.VMEM((5, 2, depth, 256), jnp.bfloat16),
            pltpu.VMEM((3, 2, 2, 2, 4, 64, 256), f32),
            pltpu.VMEM((3, 2, 2, 2, 2, 64, 256), f32),
            pltpu.VMEM((3, 2, 2, 2, 64, 256), f32),
            pltpu.VMEM((3, 2, 2, 128, 256), f32),
            pltpu.VMEM((2, 2, 2, 256, 128), f32),
            pltpu.VMEM((2, 2, 3, 2, 64, 256), f32),
            pltpu.VMEM((2, 2, 2, 4, 64, 128), f32),
            dma((6,)), dma((14,)), dma((14,)),
            dma((3, 2, 2, 2, 2)), dma((3, 2, 2, 2, 2)), dma((3, 2, 2, 2)), dma((3, 2, 2, 2)),
            dma((3, 2, 2)), dma((3, 2, 2)), dma((2, 2, 2, 4)), dma((2, 2, 2, 4)),
        ],
        compiler_params=pltpu.CompilerParams(
            collective_id=0, has_side_effects=True, vmem_limit_bytes=60 * 2**20
        ),
        cost_estimate=pl.CostEstimate(flops=16 * 10**9, bytes_accessed=8 * 10**6, transcendentals=0),
    )(own)


def solution(mesh):
    return jax.shard_map(
        shards,
        mesh=mesh,
        in_specs=(P("aux", None, "basis"),),
        out_specs=P(("basis", "aux"), None),
        check_vma=False,
    )
```

```python
import jax
import jax.numpy as jnp
from jax import lax
from jax.experimental import pallas as pl
from jax.experimental.pallas import tpu as pltpu
from jax.sharding import PartitionSpec as P

MESH = pl.DeviceIdType.MESH


def position():
    b = lax.axis_index("basis")
    a = lax.axis_index("aux")
    return b // 4, (b // 2) % 2, b % 2, a // 2, a % 2


def device(z, h, c, x, l):
    return (z * 4 + h * 2 + c, x * 2 + l)


def remote(src, dst, send, recv, who):
    return pltpu.make_async_remote_copy(
        src_ref=src, dst_ref=dst, send_sem=send, recv_sem=recv,
        device_id=who, device_id_type=MESH,
    )


def kernel(a_ref, out_ref, stage, rows, cols, hop, part, got1, got2, done, turned, byrow, bycol,
           ls, ss, rs, s1, r1, s2, r2, sr, rr, st, rt):
    z, h, c, x, l = position()
    m = 1 - l
    mate = device(z, h, c, x, m)
    other = device(z, 1 - h, c, x, m)
    cross = device(z, 1 - h, c, x, l)
    core = device(z, h, 1 - c, x, l)
    down = device((z + 3) % 4, h, c, x, l)
    up = device((z + 1) % 4, h, c, x, l)
    xa = x + 1 - 2 * (x % 2)
    xb = 3 - x
    xo = 3 - xa
    near_a = device(z, h, c, xa, l)
    near_b = device(z, h, c, xb, l)
    depth = a_ref.shape[0]
    half = rows.shape[3]
    quarter = depth // 4

    barrier = pltpu.get_barrier_semaphore()
    senders = [mate, other, cross, core, up, near_a, near_b]
    for i in (1, 2):
        for cs in range(2):
            for xs in range(4):
                senders.append(device((z + 4 - i) % 4, h, cs, xs, l))
    for who in senders:
        pl.semaphore_signal(barrier, inc=1, device_id=who, device_id_type=MESH)

    loads = [
        pltpu.make_async_copy(
            a_ref.at[pl.ds(q * quarter, quarter)], stage.at[pl.ds(q * quarter, quarter)], ls.at[q]
        )
        for q in range(4)
    ]
    for one in loads:
        one.start()
    for q in range(4):
        loads[q].wait()

        def sort(n, carry):
            at = pl.multiple_of(q * quarter + n * 128, 128)
            block = stage[pl.ds(at, 128), :]
            for g in range(2):
                rows[0, g, pl.ds(at, 128), :] = jnp.concatenate(
                    [block[:, t * 128 + g * 64 : t * 128 + g * 64 + 64] for t in range(4)], axis=1
                )
            return carry

        lax.fori_loop(0, quarter // 128, sort, 0)
    pl.semaphore_wait(barrier, len(senders))

    fours = [(q * quarter, quarter) for q in range(4)]
    parts = [(0, 2 * quarter), (2 * quarter, quarter), (3 * quarter, quarter)]

    def copies(n, src, dst, who, spans):
        return [
            remote(src.at[pl.ds(*span)], dst.at[pl.ds(*span)], ss.at[n, k], rs.at[n, k], who)
            for k, span in enumerate(spans)
        ]

    def side(n, cr):
        return cols.at[n, :, pl.ds(cr * half, half)]

    whole = [(0, depth)]
    mate1 = copies(0, rows.at[0, m], rows.at[1, m], mate, fours)
    mate2 = copies(1, rows.at[0, l], rows.at[1, l], mate, whole)
    relay2 = copies(2, rows.at[3, m], rows.at[2, m], mate, parts)
    other1 = copies(3, rows.at[0, l], rows.at[3, l], other, whole)
    relay1 = copies(4, rows.at[1, l], rows.at[2, l], other, fours)
    other2 = copies(5, rows.at[0, m], rows.at[3, m], other, parts)
    down1 = copies(6, rows.at[0, l], side(2 + l, 0), down, whole)
    down2 = copies(7, rows.at[1, l], side(2 + m, 0), down, fours)
    core1 = copies(8, rows.at[0, l], side(l, 1), core, whole)
    core2 = copies(9, rows.at[1, l], side(m, 1), core, fours)
    core3 = copies(10, side(2 + l, 0), side(2 + l, 1), core, whole)
    core4 = copies(11, side(2 + m, 0), side(2 + m, 1), core, fours)
    core5 = copies(12, side(4, 0), side(4, 1), core, fours)
    take = ((z + 2) % 4) // 2
    soon = take == l
    relay_soon = ((z + 1) % 4) // 2 == l
    lift = copies(13, rows.at[(take + l) % 2, l], hop, up, fours)
    forward = copies(14, hop, side(4, 0), up, fours)
    keep1 = pltpu.make_async_copy(rows.at[0, l], side(l, 0), ls.at[4])
    keep2 = pltpu.make_async_copy(rows.at[1, l], side(m, 0), ls.at[5])

    def start(those):
        for one in those:
            one.start()

    def arrive(those):
        for one in those:
            one.wait_recv()

    def pass_on(k):
        lift[k].wait_recv()
        forward[k].start()

    def multiply(i, hr, role, g, column, first, k=None):
        span = pl.ds(0, depth) if k is None else pl.ds(*parts[k])
        block = lax.dot_general(
            rows[role, g, span], cols[column, span], (((0,), (0,)), ((), ())),
            preferred_element_type=jnp.float32,
        )
        for cr in range(2):
            piece = block[:, cr * half : cr * half + half].reshape(4, 64, half)
            if first:
                part[i, hr, g, cr] = piece
            else:
                part[i, hr, g, cr] += piece

    def scatter1(i, hr, g):
        return [
            remote(
                part.at[i, hr, g, cr, piece], got1.at[i, hr, g, cr, k],
                s1.at[i, hr, g, cr, k], r1.at[i, hr, g, cr, k], near,
            )
            for cr, near, mine in ((0, near_a, xa), (1, near_b, xb))
            for k, piece in ((0, mine), (1, xo))
        ]

    def scatter2(i, hr, g):
        return [
            remote(
                part.at[i, hr, g, cr, piece], got2.at[i, hr, g, cr],
                s2.at[i, hr, g, cr], r2.at[i, hr, g, cr], near,
            )
            for cr, near, piece in ((0, near_b, xb), (1, near_a, xa))
        ]

    def begin(i, hr, g):
        for one in scatter1(i, hr, g):
            one.start()

    def middle(i, hr, g):
        for one in scatter1(i, hr, g):
            one.wait_recv()
        part[i, hr, g, 0, xb] += got1[i, hr, g, 0, 1]
        part[i, hr, g, 1, xa] += got1[i, hr, g, 1, 1]
        for one in scatter2(i, hr, g):
            one.start()

    def finish(i, hr, g):
        for one in scatter2(i, hr, g):
            one.wait_recv()
        for cr in range(2):
            done[i, hr, cr, pl.ds(pl.multiple_of(g * 64, 64), 64), :] = (
                part[i, hr, g, cr, x] + got1[i, hr, g, cr, 0] + got2[i, hr, g, cr]
            )

    def rowwise(i, hr, g, who):
        return remote(
            done.at[i, hr, :, pl.ds(pl.multiple_of(g * 64, 64), 64), :], byrow.at[hr, l, i],
            sr.at[i, hr, g], rr.at[i, hr, l], who,
        )

    def colwise(i, hr):
        return [
            remote(
                turned.at[i - 1, hr, cr, pl.ds(xs * 64, 64)], bycol.at[i - 1, hr, c, x],
                st.at[i - 1, hr, cr, xs], rt.at[i - 1, hr, c, x],
                device((z + i) % 4, h, (c + cr) % 2, xs, l),
            )
            for cr in range(2)
            for xs in range(4)
        ]

    def turn(i, hr):
        for cr in range(2):
            turned[i - 1, hr, cr] = done[i, hr, cr].T
        for one in colwise(i, hr):
            one.start()

    late = (z // 2 + l) % 2

    start(mate1 + other1 + down1 + core1 + mate2)
    keep1.start()

    @pl.when(soon)
    def _():
        start(lift)

    for k in range(4):
        if k == 1:
            keep1.wait()
            arrive(core1)
            multiply(0, 0, 0, l, l, True)
        if k == 2:
            multiply(0, 0, 0, m, l, True)
        mate1[k].wait_recv()
        down2[k].start()
        relay1[k].start()
        core2[k].start()

        @pl.when(jnp.logical_not(soon))
        def _():
            lift[k].start()

        @pl.when(relay_soon)
        def _():
            pass_on(k)

    keep2.start()
    arrive(other1)
    start(relay2 + other2)
    arrive(down1)
    start(core3)
    keep2.wait()
    arrive(core2)
    multiply(0, 0, 1, l, m, False)
    begin(0, 0, l)
    multiply(0, 1, 3, m, m, True)
    arrive(core3)
    multiply(1, 0, 0, l, 2 + l, True)
    multiply(1, 0, 0, m, 2 + l, True)
    middle(0, 0, l)
    for k in range(2):
        @pl.when(jnp.logical_not(relay_soon))
        def _():
            pass_on(k)

    for k in range(3):
        down2[k].wait_recv()
        core4[k].start()
    finish(0, 0, l)

    arrive(mate2)
    multiply(0, 0, 1, m, m, False)
    begin(0, 0, m)
    arrive(relay1)
    multiply(0, 1, 2, m, l, False)
    begin(0, 1, m)
    down2[3].wait_recv()
    core4[3].start()
    multiply(1, 1, 2, m, 2 + l, True)

    @pl.when(jnp.logical_not(relay_soon))
    def _():
        pass_on(2)

    arrive(core4)
    multiply(1, 0, 1, l, 2 + m, False)
    begin(1, 0, l)
    multiply(1, 0, 1, m, 2 + m, False)
    begin(1, 0, m)
    multiply(1, 1, 3, m, 2 + m, False)
    begin(1, 1, m)
    middle(0, 0, m)
    middle(0, 1, m)
    for k in range(2):
        forward[k].wait_recv()
        core5[k].start()

    @pl.when(jnp.logical_not(relay_soon))
    def _():
        pass_on(3)

    middle(1, 0, l)
    for k in range(2, 4):
        forward[k].wait_recv()
        core5[k].start()
    middle(1, 0, m)
    arrive(core5)
    multiply(2, 0, late, l, 4, True)
    begin(2, 0, l)
    multiply(2, 0, late, m, 4, True)
    begin(2, 0, m)
    multiply(2, 1, 2 + late, m, 4, True)
    begin(2, 1, m)
    middle(1, 1, m)
    finish(1, 0, l)
    finish(1, 0, m)
    turn(1, 0)

    for k in range(3):
        other2[k].wait_recv()
        relay2[k].wait_recv()
        if k == 2:
            rowwise(0, 0, m, mate).start()
            rowwise(0, 1, m, other).start()
            rowwise(1, 0, m, mate).start()
            rowwise(1, 1, m, other).start()
        multiply(1, 1, 3, l, 2 + m, k == 0, k)
        multiply(1, 1, 2, l, 2 + l, False, k)
        if k == 2:
            begin(1, 1, l)
        multiply(2, 1, 2 + late, l, 4, k == 0, k)
        if k == 2:
            begin(2, 1, l)
        multiply(0, 1, 3, l, m, k == 0, k)
        multiply(0, 1, 2, l, l, False, k)
        if k == 0:
            finish(0, 0, m)
            finish(0, 1, m)
            middle(2, 0, l)
        if k == 1:
            middle(2, 0, m)
            finish(1, 1, m)
    begin(0, 1, l)
    middle(2, 1, m)
    finish(2, 0, l)
    finish(2, 0, m)
    rowwise(2, 0, m, mate).start()
    turn(2, 0)
    middle(1, 1, l)
    finish(2, 1, m)
    rowwise(2, 1, m, other).start()
    middle(2, 1, l)
    middle(0, 1, l)
    finish(1, 1, l)
    rowwise(1, 1, l, cross).start()
    turn(1, 1)
    finish(2, 1, l)
    rowwise(2, 1, l, cross).start()
    turn(2, 1)
    finish(0, 1, l)
    rowwise(0, 1, l, cross).start()

    def place(zs, hs, cs, at):
        return pl.ds(pl.multiple_of(zs * 2048 + hs * 1024 + cs * 512 + at, 128), 128)

    for i in range(3):
        for cr in range(2):
            byrow[0, l, i, cr] = done[i, 0, cr, pl.ds(pl.multiple_of(l * 64, 64), 64), :]
    low = lax.broadcasted_iota(jnp.int32, (64, 128), 1) < 64
    for hr in range(2):
        for i in (1, 2):
            for cs in range(2):
                for xs in range(4):
                    remote(
                        turned.at[i - 1, hr, 0, pl.ds(0, 64)], bycol.at[i - 1, hr, cs, xs],
                        st.at[i - 1, hr, 0, 0], rt.at[i - 1, hr, cs, xs], mate,
                    ).wait_recv()
                    out_ref[:, place((z + 4 - i) % 4, (h + hr) % 2, cs, xs * 128)] = bycol[i - 1, hr, cs, xs]
        for i in (1, 2, 0):
            for g in (m,) if hr == 0 else (0, 1):
                remote(byrow.at[hr, g, i], byrow.at[hr, g, i], sr.at[i, hr, g], rr.at[i, hr, g], mate).wait_recv()
            for cr in range(2):
                for t in range(2):
                    v0 = byrow[hr, 0, i, cr, :, t * 128 : t * 128 + 128]
                    v1 = byrow[hr, 1, i, cr, :, t * 128 : t * 128 + 128]
                    even = jnp.where(low, v0, pltpu.roll(v1, 64, 1))
                    odd = jnp.where(low, pltpu.roll(v0, 64, 1), v1)
                    for value, xs in ((even, 2 * t), (odd, 2 * t + 1)):
                        where = place((z + i) % 4, (h + hr) % 2, (c + cr) % 2, xs * 128)
                        if i == 2:
                            out_ref[:, where] += value
                        else:
                            out_ref[:, where] = value

    for one in (mate1 + mate2 + relay2 + other1 + relay1 + other2 + down1 + down2 + core1 + core2 + core3
                + core4 + core5 + lift + forward):
        one.wait_send()
    for i in range(3):
        for hr in range(2):
            for g in range(2):
                for one in scatter1(i, hr, g) + scatter2(i, hr, g):
                    one.wait_send()
                if hr == 1:
                    rowwise(i, 1, g, cross).wait_send()
            if hr == 0:
                rowwise(i, 0, m, mate).wait_send()
            if i:
                for one in colwise(i, hr):
                    one.wait_send()


def shards(three_index):
    depth = three_index.shape[0] * three_index.shape[1]
    own = three_index.reshape(depth, 512)
    dma = pltpu.SemaphoreType.DMA
    f32 = jnp.float32
    return pl.pallas_call(
        kernel,
        out_shape=jax.ShapeDtypeStruct((64, 8192), f32),
        in_specs=[pl.BlockSpec(memory_space=pl.ANY)],
        out_specs=pl.BlockSpec(memory_space=pltpu.VMEM),
        scratch_shapes=[
            pltpu.VMEM((depth, 512), jnp.bfloat16),
            pltpu.VMEM((4, 2, depth, 256), jnp.bfloat16),
            pltpu.VMEM((5, depth, 512), jnp.bfloat16),
            pltpu.VMEM((depth, 256), jnp.bfloat16),
            pltpu.VMEM((3, 2, 2, 2, 4, 64, 256), f32),
            pltpu.VMEM((3, 2, 2, 2, 2, 64, 256), f32),
            pltpu.VMEM((3, 2, 2, 2, 64, 256), f32),
            pltpu.VMEM((3, 2, 2, 128, 256), f32),
            pltpu.VMEM((2, 2, 2, 256, 128), f32),
            pltpu.VMEM((2, 2, 3, 2, 64, 256), f32),
            pltpu.VMEM((2, 2, 2, 4, 64, 128), f32),
            dma((6,)), dma((15, 4)), dma((15, 4)),
            dma((3, 2, 2, 2, 2)), dma((3, 2, 2, 2, 2)), dma((3, 2, 2, 2)), dma((3, 2, 2, 2)),
            dma((3, 2, 2)), dma((3, 2, 2)), dma((2, 2, 2, 4)), dma((2, 2, 2, 4)),
        ],
        compiler_params=pltpu.CompilerParams(
            collective_id=0, has_side_effects=True, vmem_limit_bytes=60 * 2**20
        ),
        cost_estimate=pl.CostEstimate(flops=16 * 10**9, bytes_accessed=8 * 10**6, transcendentals=0),
    )(own)


def solution(mesh):
    return jax.shard_map(
        shards,
        mesh=mesh,
        in_specs=(P("aux", None, "basis"),),
        out_specs=P(("basis", "aux"), None),
        check_vma=False,
    )
```

```python
import jax
import jax.numpy as jnp
from jax import lax
from jax.experimental import pallas as pl
from jax.experimental.pallas import tpu as pltpu
from jax.sharding import PartitionSpec as P

MESH = pl.DeviceIdType.MESH


def position():
    b = lax.axis_index("basis")
    a = lax.axis_index("aux")
    return b // 4, (b // 2) % 2, b % 2, a // 2, a % 2


def device(z, h, c, x, l):
    return (z * 4 + h * 2 + c, x * 2 + l)


def remote(src, dst, send, recv, who):
    return pltpu.make_async_remote_copy(
        src_ref=src, dst_ref=dst, send_sem=send, recv_sem=recv,
        device_id=who, device_id_type=MESH,
    )


LEVELS = 10
SPREAD = 256.0 * LEVELS


def encode(value, ref):
    rest = []
    for k in range(2):
        one = value[32 * k : 32 * k + 32]
        high = one.astype(jnp.bfloat16)
        ref[32 * k : 32 * k + 32] = high
        high = high.astype(jnp.float32)
        scale = SPREAD * pl.reciprocal(jnp.maximum(jnp.abs(high), 1e-30), approx=True)
        rest.append(jnp.floor((one - high) * scale + 0.5))
    ref[64:96] = (rest[0] * (2 * LEVELS + 1) + rest[1]).astype(jnp.bfloat16)


def decode(ref):
    both = ref[64:96].astype(jnp.float32)
    first = jnp.floor(both * (1.0 / (2 * LEVELS + 1)) + 0.5)
    out = []
    for k, rest in enumerate((first, both - first * (2 * LEVELS + 1))):
        high = ref[32 * k : 32 * k + 32].astype(jnp.float32)
        out.append(high + jnp.abs(high) * (rest * (1.0 / SPREAD)))
    return jnp.concatenate(out, axis=0)


def kernel(a_ref, out_ref, stage, rows, cols, hop, part, put1, put2, got1, got2, done, turned, packed, byrow, bycol,
           bits, ls, ss, rs, s1, r1, s2, r2, sr, rr, st, rt):
    z, h, c, x, l = position()
    m = 1 - l
    mate = device(z, h, c, x, m)
    other = device(z, 1 - h, c, x, m)
    cross = device(z, 1 - h, c, x, l)
    core = device(z, h, 1 - c, x, l)
    down = device((z + 3) % 4, h, c, x, l)
    up = device((z + 1) % 4, h, c, x, l)
    xa = x + 1 - 2 * (x % 2)
    xb = 3 - x
    xo = 3 - xa
    near_a = device(z, h, c, xa, l)
    near_b = device(z, h, c, xb, l)
    depth = a_ref.shape[0]
    half = rows.shape[3]
    quarter = depth // 4

    barrier = pltpu.get_barrier_semaphore()
    senders = [mate, other, cross, core, up, near_a, near_b]
    for i in (1, 2):
        for cs in range(2):
            for xs in range(4):
                senders.append(device((z + 4 - i) % 4, h, cs, xs, l))
    for who in senders:
        pl.semaphore_signal(barrier, inc=1, device_id=who, device_id_type=MESH)

    loads = [
        pltpu.make_async_copy(
            a_ref.at[pl.ds(q * quarter, quarter)], stage.at[pl.ds(q * quarter, quarter)], ls.at[q]
        )
        for q in range(4)
    ]
    for one in loads:
        one.start()
    def sort(q):
        loads[q].wait()

        def body(n, carry):
            at = pl.multiple_of(q * quarter + n * 128, 128)
            block = stage[pl.ds(at, 128), :]
            for g in range(2):
                rows[0, g, pl.ds(at, 128), :] = jnp.concatenate(
                    [block[:, t * 128 + g * 64 : t * 128 + g * 64 + 64] for t in range(4)], axis=1
                )
            return carry

        lax.fori_loop(0, quarter // 128, body, 0)

    fours = [(q * quarter, quarter) for q in range(4)]
    parts = [(0, 2 * quarter), (2 * quarter, quarter), (3 * quarter, quarter)]

    def copies(n, src, dst, who, spans):
        return [
            remote(src.at[pl.ds(*span)], dst.at[pl.ds(*span)], ss.at[n, k], rs.at[n, k], who)
            for k, span in enumerate(spans)
        ]

    def side(n, cr):
        return cols.at[n, :, pl.ds(cr * half, half)]

    whole = [(0, depth)]
    mate1 = copies(0, rows.at[0, m], rows.at[1, m], mate, fours)
    mate2 = copies(1, rows.at[0, l], rows.at[1, l], mate, whole)
    relay2 = copies(2, rows.at[3, m], rows.at[2, m], mate, parts)
    other1 = copies(3, rows.at[0, l], rows.at[3, l], other, fours)
    relay1 = copies(4, rows.at[1, l], rows.at[2, l], other, fours)
    other2 = copies(5, rows.at[0, m], rows.at[3, m], other, parts)
    down1 = copies(6, rows.at[0, l], side(2 + l, 0), down, whole)
    down2 = copies(7, rows.at[1, l], side(2 + m, 0), down, fours)
    core1 = copies(8, rows.at[0, l], side(l, 1), core, whole)
    core2 = copies(9, rows.at[1, l], side(m, 1), core, fours)
    core3 = copies(10, side(2 + l, 0), side(2 + l, 1), core, whole)
    core4 = copies(11, side(2 + m, 0), side(2 + m, 1), core, fours)
    core5 = copies(12, side(4, 0), side(4, 1), core, fours)
    take = ((z + 2) % 4) // 2
    soon = take == l
    relay_soon = ((z + 1) % 4) // 2 == l
    lift = copies(13, rows.at[(take + l) % 2, l], hop, up, fours)
    forward = copies(14, hop, side(4, 0), up, fours)
    keep1 = pltpu.make_async_copy(rows.at[0, l], side(l, 0), ls.at[4])
    keep2 = pltpu.make_async_copy(rows.at[1, l], side(m, 0), ls.at[5])
    core6 = copies(15, rows.at[0, m], side(5, 1), core, whole)
    core7 = copies(16, rows.at[1, m], side(6, 1), core, whole)
    keep3 = pltpu.make_async_copy(rows.at[0, m], side(5, 0), ls.at[6])
    keep4 = pltpu.make_async_copy(rows.at[1, m], side(6, 0), ls.at[7])

    def start(those):
        for one in those:
            one.start()

    def arrive(those):
        for one in those:
            one.wait_recv()

    def pass_on(k):
        lift[k].wait_recv()
        forward[k].start()

    def multiply(i, hr, role, g, column, first, k=None, to=None):
        span = pl.ds(0, depth) if k is None else pl.ds(*parts[k])
        block = lax.dot_general(
            rows[role, g, span], cols[column, span], (((0,), (0,)), ((), ())),
            preferred_element_type=jnp.float32,
        )
        for cr in range(2):
            piece = block[:, cr * half : cr * half + half].reshape(4, 64, half)
            if first:
                part[i, hr, g if to is None else to, cr] = piece
            else:
                part[i, hr, g if to is None else to, cr] += piece

    def scatter1(i, hr, g):
        return [
            remote(
                put1.at[i, hr, g, cr, k], got1.at[i, hr, g, cr, k],
                s1.at[i, hr, g, cr, k], r1.at[i, hr, g, cr, k], near,
            )
            for cr, near in ((0, near_a), (1, near_b))
            for k in range(2)
        ]

    def scatter2(i, hr, g):
        return [
            remote(
                put2.at[i, hr, g, cr], got2.at[i, hr, g, cr],
                s2.at[i, hr, g, cr], r2.at[i, hr, g, cr], near,
            )
            for cr, near in ((0, near_b), (1, near_a))
        ]

    def begin(i, hr, g):
        for cr, mine in ((0, xa), (1, xb)):
            for k, piece in ((0, mine), (1, xo)):
                encode(part[i, hr, g, cr, piece], put1.at[i, hr, g, cr, k])
        for one in scatter1(i, hr, g):
            one.start()

    def middle(i, hr, g):
        for one in scatter1(i, hr, g):
            one.wait_recv()
        for cr, piece in ((0, xb), (1, xa)):
            encode(part[i, hr, g, cr, piece] + decode(got1.at[i, hr, g, cr, 1]), put2.at[i, hr, g, cr])
        for one in scatter2(i, hr, g):
            one.start()

    def finish(i, hr, g):
        for one in scatter2(i, hr, g):
            one.wait_recv()
        for cr in range(2):
            done[i, hr, cr, pl.ds(pl.multiple_of(g * 64, 64), 64), :] = (
                part[i, hr, g, cr, x] + decode(got1.at[i, hr, g, cr, 0]) + decode(got2.at[i, hr, g, cr])
            )

    def rowwise(i, hr, g, who, half_of=l):
        return remote(
            done.at[i, hr, :, pl.ds(pl.multiple_of(g * 64, 64), 64), :], byrow.at[hr, half_of, i],
            sr.at[i, hr, g], rr.at[i, hr, half_of], who,
        )

    def rowwise_diagonal():
        return rowwise(0, 1, l, other, m)

    def colwise(i):
        return [
            remote(
                turned.at[i - 1, cr, pl.ds(xs * 64, 64)], bycol.at[i - 1, c, x],
                st.at[i - 1, 0, cr, xs], rt.at[i - 1, 0, c, x],
                device((z + i) % 4, h, (c + cr) % 2, xs, l),
            )
            for cr in range(2)
            for xs in range(4)
        ]

    def colwise_half(i, g):
        return [
            remote(
                packed.at[i - 1, g, cr, xs], bits.at[i - 1, g, c, x],
                st.at[i - 1, 1 + g, cr, xs], rt.at[i - 1, 1 + g, c, x],
                device((z + i) % 4, h, (c + cr) % 2, xs, l),
            )
            for cr in range(2)
            for xs in range(4)
        ]

    def turn(i):
        for cr in range(2):
            turned[i - 1, cr] = done[i, 0, cr].T
        start(colwise(i))

    def turn_half(i, g):
        for cr in range(2):
            block = done[i, 1, cr, pl.ds(pl.multiple_of(g * 64, 64), 64), :].T
            for xs in range(4):
                packed[i - 1, g, cr, xs] = jnp.concatenate(
                    [block[xs * 64 : xs * 64 + 32], block[xs * 64 + 32 : xs * 64 + 64]], axis=1
                )
        start(colwise_half(i, g))

    late = (z // 2 + l) % 2

    for q in range(4):
        sort(q)
        if q == 0:
            pl.semaphore_wait(barrier, len(senders))
        mate1[q].start()
        other1[q].start()

        @pl.when(soon)
        def _():
            lift[q].start()

    start(down1 + core1 + mate2 + core6)
    keep1.start()
    keep3.start()

    for k in range(4):
        if k == 1:
            keep1.wait()
            arrive(core1)
            multiply(0, 0, 0, l, l, True)
        if k == 2:
            multiply(0, 0, 0, m, l, True)
        mate1[k].wait_recv()
        down2[k].start()
        relay1[k].start()
        core2[k].start()

        @pl.when(jnp.logical_not(soon))
        def _():
            lift[k].start()

        @pl.when(relay_soon)
        def _():
            pass_on(k)

    keep2.start()
    arrive(other1)
    start(relay2 + other2)
    arrive(down1)
    start(core3)
    keep2.wait()
    arrive(core2)
    multiply(0, 0, 1, l, m, False)
    begin(0, 0, l)
    multiply(0, 1, 3, m, m, True)
    arrive(core3)
    multiply(1, 0, 0, l, 2 + l, True)
    multiply(1, 0, 0, m, 2 + l, True)
    middle(0, 0, l)
    for k in range(2):
        @pl.when(jnp.logical_not(relay_soon))
        def _():
            pass_on(k)

    for k in range(3):
        down2[k].wait_recv()
        core4[k].start()
    finish(0, 0, l)

    arrive(mate2)
    keep4.start()
    start(core7)
    multiply(0, 0, 1, m, m, False)
    begin(0, 0, m)
    arrive(relay1)
    multiply(0, 1, 2, m, l, False)
    begin(0, 1, m)
    keep3.wait()
    arrive(core6)
    multiply(0, 1, 2, m, 5, True, to=l)
    down2[3].wait_recv()
    core4[3].start()
    multiply(1, 1, 2, m, 2 + l, True)

    @pl.when(jnp.logical_not(relay_soon))
    def _():
        pass_on(2)

    arrive(core4)
    multiply(1, 0, 1, l, 2 + m, False)
    begin(1, 0, l)
    multiply(1, 0, 1, m, 2 + m, False)
    begin(1, 0, m)
    multiply(1, 1, 3, m, 2 + m, False)
    begin(1, 1, m)
    keep4.wait()
    arrive(core7)
    multiply(0, 1, 3, m, 6, False, to=l)
    begin(0, 1, l)
    middle(0, 0, m)
    middle(0, 1, m)
    for k in range(2):
        forward[k].wait_recv()
        core5[k].start()

    @pl.when(jnp.logical_not(relay_soon))
    def _():
        pass_on(3)

    middle(1, 0, l)
    for k in range(2, 4):
        forward[k].wait_recv()
        core5[k].start()
    middle(1, 0, m)
    arrive(core5)
    multiply(2, 0, late, l, 4, True)
    begin(2, 0, l)
    multiply(2, 0, late, m, 4, True)
    begin(2, 0, m)
    multiply(2, 1, 2 + late, m, 4, True)
    begin(2, 1, m)
    middle(1, 1, m)
    finish(1, 0, l)
    finish(1, 0, m)
    turn(1)
    middle(0, 1, l)
    finish(1, 1, m)
    turn_half(1, m)

    for k in range(3):
        other2[k].wait_recv()
        relay2[k].wait_recv()
        multiply(1, 1, 3, l, 2 + m, k == 0, k)
        multiply(1, 1, 2, l, 2 + l, False, k)
        if k == 2:
            begin(1, 1, l)
        multiply(2, 1, 2 + late, l, 4, k == 0, k)
        if k == 0:
            finish(0, 0, m)
            finish(0, 1, m)
            middle(2, 0, l)
        if k == 1:
            middle(2, 0, m)
            finish(0, 1, l)
            middle(2, 1, m)
    begin(2, 1, l)
    rowwise(0, 0, m, mate).start()
    rowwise(0, 1, m, other).start()
    rowwise(1, 0, m, mate).start()
    rowwise(1, 1, m, other).start()
    rowwise_diagonal().start()
    finish(2, 0, l)
    finish(2, 0, m)
    rowwise(2, 0, m, mate).start()
    turn(2)
    finish(2, 1, m)
    rowwise(2, 1, m, other).start()
    turn_half(2, m)
    middle(1, 1, l)
    middle(2, 1, l)
    finish(1, 1, l)
    rowwise(1, 1, l, cross).start()
    turn_half(1, l)
    finish(2, 1, l)
    rowwise(2, 1, l, cross).start()
    turn_half(2, l)

    def place(zs, hs, cs, at):
        return pl.ds(pl.multiple_of(zs * 2048 + hs * 1024 + cs * 512 + at, 128), 128)

    for i in range(3):
        for cr in range(2):
            byrow[0, l, i, cr] = done[i, 0, cr, pl.ds(pl.multiple_of(l * 64, 64), 64), :]
    low = lax.broadcasted_iota(jnp.int32, (64, 128), 1) < 64
    for hr in range(2):
        for i in (1, 2):
            for cs in range(2):
                for xs in range(4):
                    where = place((z + 4 - i) % 4, (h + hr) % 2, cs, xs * 128)
                    if hr == 0:
                        remote(
                            bycol.at[i - 1, cs, xs], bycol.at[i - 1, cs, xs],
                            st.at[i - 1, 0, 0, 0], rt.at[i - 1, 0, cs, xs], mate,
                        ).wait_recv()
                        out_ref[:, where] = bycol[i - 1, cs, xs]
                    else:
                        for g in range(2):
                            remote(
                                bits.at[i - 1, g, cs, xs], bits.at[i - 1, g, cs, xs],
                                st.at[i - 1, 1 + g, 0, 0], rt.at[i - 1, 1 + g, cs, xs], mate,
                            ).wait_recv()
                        v0 = bits[i - 1, 0, cs, xs]
                        v1 = bits[i - 1, 1, cs, xs]
                        out_ref[0:32, where] = jnp.where(low[:32], v0, pltpu.roll(v1, 64, 1))
                        out_ref[32:64, where] = jnp.where(low[:32], pltpu.roll(v0, 64, 1), v1)
        for i in (1, 2, 0):
            for g in (m,) if hr == 0 else (0, 1):
                remote(byrow.at[hr, g, i], byrow.at[hr, g, i], sr.at[i, hr, g], rr.at[i, hr, g], mate).wait_recv()
            for cr in range(2):
                for t in range(2):
                    v0 = byrow[hr, 0, i, cr, :, t * 128 : t * 128 + 128]
                    v1 = byrow[hr, 1, i, cr, :, t * 128 : t * 128 + 128]
                    even = jnp.where(low, v0, pltpu.roll(v1, 64, 1))
                    odd = jnp.where(low, pltpu.roll(v0, 64, 1), v1)
                    for value, xs in ((even, 2 * t), (odd, 2 * t + 1)):
                        where = place((z + i) % 4, (h + hr) % 2, (c + cr) % 2, xs * 128)
                        if i == 2:
                            out_ref[:, where] += value
                        else:
                            out_ref[:, where] = value

    for one in (mate1 + mate2 + relay2 + other1 + relay1 + other2 + down1 + down2 + core1 + core2 + core3
                + core4 + core5 + core6 + core7 + lift + forward):
        one.wait_send()
    for i in range(3):
        for hr in range(2):
            for g in range(2):
                for one in scatter1(i, hr, g) + scatter2(i, hr, g):
                    one.wait_send()
                if hr == 1:
                    rowwise(i, 1, g, cross).wait_send()
            if hr == 0:
                rowwise(i, 0, m, mate).wait_send()
            if i:
                for one in colwise(i) if hr == 0 else colwise_half(i, 0) + colwise_half(i, 1):
                    one.wait_send()


def shards(three_index):
    depth = three_index.shape[0] * three_index.shape[1]
    own = three_index.reshape(depth, 512)
    dma = pltpu.SemaphoreType.DMA
    f32 = jnp.float32
    return pl.pallas_call(
        kernel,
        out_shape=jax.ShapeDtypeStruct((64, 8192), f32),
        in_specs=[pl.BlockSpec(memory_space=pl.ANY)],
        out_specs=pl.BlockSpec(memory_space=pltpu.VMEM),
        scratch_shapes=[
            pltpu.VMEM((depth, 512), jnp.bfloat16),
            pltpu.VMEM((4, 2, depth, 256), jnp.bfloat16),
            pltpu.VMEM((7, depth, 512), jnp.bfloat16),
            pltpu.VMEM((depth, 256), jnp.bfloat16),
            pltpu.VMEM((3, 2, 2, 2, 4, 64, 256), f32),
            pltpu.VMEM((3, 2, 2, 2, 2, 96, 256), jnp.bfloat16),
            pltpu.VMEM((3, 2, 2, 2, 96, 256), jnp.bfloat16),
            pltpu.VMEM((3, 2, 2, 2, 2, 96, 256), jnp.bfloat16),
            pltpu.VMEM((3, 2, 2, 2, 96, 256), jnp.bfloat16),
            pltpu.VMEM((3, 2, 2, 128, 256), f32),
            pltpu.VMEM((2, 2, 256, 128), f32),
            pltpu.VMEM((2, 2, 2, 4, 32, 128), f32),
            pltpu.VMEM((2, 2, 3, 2, 64, 256), f32),
            pltpu.VMEM((2, 2, 4, 64, 128), f32),
            pltpu.VMEM((2, 2, 2, 4, 32, 128), f32),
            dma((8,)), dma((17, 4)), dma((17, 4)),
            dma((3, 2, 2, 2, 2)), dma((3, 2, 2, 2, 2)), dma((3, 2, 2, 2)), dma((3, 2, 2, 2)),
            dma((3, 2, 2)), dma((3, 2, 2)), dma((2, 3, 2, 4)), dma((2, 3, 2, 4)),
        ],
        compiler_params=pltpu.CompilerParams(
            collective_id=0, has_side_effects=True, vmem_limit_bytes=60 * 2**20
        ),
        cost_estimate=pl.CostEstimate(flops=16 * 10**9, bytes_accessed=8 * 10**6, transcendentals=0),
    )(own)


def solution(mesh):
    return jax.shard_map(
        shards,
        mesh=mesh,
        in_specs=(P("aux", None, "basis"),),
        out_specs=P(("basis", "aux"), None),
        check_vma=False,
    )
```

```python
import jax
import jax.numpy as jnp
from jax import lax
from jax.experimental import pallas as pl
from jax.experimental.pallas import tpu as pltpu
from jax.sharding import PartitionSpec as P

MESH = pl.DeviceIdType.MESH


def position():
    b = lax.axis_index("basis")
    a = lax.axis_index("aux")
    return b // 4, (b // 2) % 2, b % 2, a // 2, a % 2


def device(z, h, c, x, l):
    return (z * 4 + h * 2 + c, x * 2 + l)


def remote(src, dst, send, recv, who):
    return pltpu.make_async_remote_copy(
        src_ref=src, dst_ref=dst, send_sem=send, recv_sem=recv,
        device_id=who, device_id_type=MESH,
    )


LEVELS = 10
SPREAD = 256.0 * LEVELS


def encode(value, ref):
    rest = []
    for k in range(2):
        one = value[32 * k : 32 * k + 32]
        high = one.astype(jnp.bfloat16)
        ref[32 * k : 32 * k + 32] = high
        high = high.astype(jnp.float32)
        scale = SPREAD * pl.reciprocal(jnp.maximum(jnp.abs(high), 1e-30), approx=True)
        rest.append(jnp.floor((one - high) * scale + 0.5))
    ref[64:96] = (rest[0] * (2 * LEVELS + 1) + rest[1]).astype(jnp.bfloat16)


def decode(ref):
    both = ref[64:96].astype(jnp.float32)
    first = jnp.floor(both * (1.0 / (2 * LEVELS + 1)) + 0.5)
    out = []
    for k, rest in enumerate((first, both - first * (2 * LEVELS + 1))):
        high = ref[32 * k : 32 * k + 32].astype(jnp.float32)
        out.append(high + jnp.abs(high) * (rest * (1.0 / SPREAD)))
    return jnp.concatenate(out, axis=0)


def kernel(a_ref, out_ref, stage, rows, cols, hop, part, put1, put2, got1, got2, done, turned, packed, byrow, bycol,
           bits, ls, ss, rs, s1, r1, s2, r2, sr, rr, st, rt):
    z, h, c, x, l = position()
    m = 1 - l
    mate = device(z, h, c, x, m)
    other = device(z, 1 - h, c, x, m)
    cross = device(z, 1 - h, c, x, l)
    core = device(z, h, 1 - c, x, l)
    down = device((z + 3) % 4, h, c, x, l)
    up = device((z + 1) % 4, h, c, x, l)
    xa = x + 1 - 2 * (x % 2)
    xb = 3 - x
    xo = 3 - xa
    near_a = device(z, h, c, xa, l)
    near_b = device(z, h, c, xb, l)
    depth = a_ref.shape[0]
    half = rows.shape[3]
    quarter = depth // 4

    barrier = pltpu.get_barrier_semaphore()
    senders = [mate, other, cross, core, up, near_a, near_b]
    for i in (1, 2):
        for cs in range(2):
            for xs in range(4):
                senders.append(device((z + 4 - i) % 4, h, cs, xs, l))
    for who in senders:
        pl.semaphore_signal(barrier, inc=1, device_id=who, device_id_type=MESH)

    loads = [
        pltpu.make_async_copy(
            a_ref.at[pl.ds(q * quarter, quarter)], stage.at[pl.ds(q * quarter, quarter)], ls.at[q]
        )
        for q in range(4)
    ]
    for one in loads:
        one.start()
    def sort(q):
        loads[q].wait()

        def body(n, carry):
            at = pl.multiple_of(q * quarter + n * 128, 128)
            block = stage[pl.ds(at, 128), :]
            for g in range(2):
                rows[0, g, pl.ds(at, 128), :] = jnp.concatenate(
                    [block[:, t * 128 + g * 64 : t * 128 + g * 64 + 64] for t in range(4)], axis=1
                )
            return carry

        lax.fori_loop(0, quarter // 128, body, 0)

    fours = [(q * quarter, quarter) for q in range(4)]
    parts = [(0, 2 * quarter), (2 * quarter, quarter), (3 * quarter, quarter)]

    def copies(n, src, dst, who, spans):
        return [
            remote(src.at[pl.ds(*span)], dst.at[pl.ds(*span)], ss.at[n, k], rs.at[n, k], who)
            for k, span in enumerate(spans)
        ]

    def side(n, cr):
        return cols.at[n, :, pl.ds(cr * half, half)]

    whole = [(0, depth)]
    mate1 = copies(0, rows.at[0, m], rows.at[1, m], mate, fours)
    mate2 = copies(1, rows.at[0, l], rows.at[1, l], mate, whole)
    relay2 = copies(2, rows.at[3, m], rows.at[2, m], mate, parts)
    other1 = copies(3, rows.at[0, l], rows.at[3, l], other, fours)
    relay1 = copies(4, rows.at[1, l], rows.at[2, l], other, fours)
    other2 = copies(5, rows.at[0, m], rows.at[3, m], other, parts)
    down1 = copies(6, rows.at[0, l], side(2 + l, 0), down, whole)
    down2 = copies(7, rows.at[1, l], side(2 + m, 0), down, fours)
    core1 = copies(8, rows.at[0, l], side(l, 1), core, whole)
    core2 = copies(9, rows.at[1, l], side(m, 1), core, fours)
    core3 = copies(10, side(2 + l, 0), side(2 + l, 1), core, whole)
    core4 = copies(11, side(2 + m, 0), side(2 + m, 1), core, fours)
    core5 = copies(12, side(4, 0), side(4, 1), core, fours)
    take = ((z + 2) % 4) // 2
    soon = take == l
    relay_soon = ((z + 1) % 4) // 2 == l
    lift = copies(13, rows.at[(take + l) % 2, l], hop, up, fours)
    forward = copies(14, hop, side(4, 0), up, fours)
    keep1 = pltpu.make_async_copy(rows.at[0, l], side(l, 0), ls.at[4])
    keep2 = pltpu.make_async_copy(rows.at[1, l], side(m, 0), ls.at[5])
    core6 = copies(15, rows.at[0, m], side(5, 1), core, whole)
    core7 = copies(16, rows.at[1, m], side(6, 1), core, whole)
    keep3 = pltpu.make_async_copy(rows.at[0, m], side(5, 0), ls.at[6])
    keep4 = pltpu.make_async_copy(rows.at[1, m], side(6, 0), ls.at[7])

    def start(those):
        for one in those:
            one.start()

    def arrive(those):
        for one in those:
            one.wait_recv()

    def pass_on(k):
        lift[k].wait_recv()
        forward[k].start()

    def multiply(i, hr, role, g, column, first, k=None, to=None):
        span = pl.ds(0, depth) if k is None else pl.ds(*parts[k])
        block = lax.dot_general(
            rows[role, g, span], cols[column, span], (((0,), (0,)), ((), ())),
            preferred_element_type=jnp.float32,
        )
        for cr in range(2):
            piece = block[:, cr * half : cr * half + half].reshape(4, 64, half)
            if first:
                part[i, hr, g if to is None else to, cr] = piece
            else:
                part[i, hr, g if to is None else to, cr] += piece

    def scatter1(i, hr, g):
        return [
            remote(
                put1.at[i, hr, g, cr, k], got1.at[i, hr, g, cr, k],
                s1.at[i, hr, g, cr, k], r1.at[i, hr, g, cr, k], near,
            )
            for cr, near in ((0, near_a), (1, near_b))
            for k in range(2)
        ]

    def scatter2(i, hr, g):
        return [
            remote(
                put2.at[i, hr, g, cr], got2.at[i, hr, g, cr],
                s2.at[i, hr, g, cr], r2.at[i, hr, g, cr], near,
            )
            for cr, near in ((0, near_b), (1, near_a))
        ]

    def begin(i, hr, g):
        for cr, mine in ((0, xa), (1, xb)):
            for k, piece in ((0, mine), (1, xo)):
                encode(part[i, hr, g, cr, piece], put1.at[i, hr, g, cr, k])
        for one in scatter1(i, hr, g):
            one.start()

    def middle(i, hr, g):
        for one in scatter1(i, hr, g):
            one.wait_recv()
        for cr, piece in ((0, xb), (1, xa)):
            encode(part[i, hr, g, cr, piece] + decode(got1.at[i, hr, g, cr, 1]), put2.at[i, hr, g, cr])
        for one in scatter2(i, hr, g):
            one.start()

    def finish(i, hr, g):
        for one in scatter2(i, hr, g):
            one.wait_recv()
        for cr in range(2):
            done[i, hr, cr, pl.ds(pl.multiple_of(g * 64, 64), 64), :] = (
                part[i, hr, g, cr, x] + decode(got1.at[i, hr, g, cr, 0]) + decode(got2.at[i, hr, g, cr])
            )

    def rowwise(i, hr, g, who, half_of=l):
        return remote(
            done.at[i, hr, :, pl.ds(pl.multiple_of(g * 64, 64), 64), :], byrow.at[hr, half_of, i],
            sr.at[i, hr, g], rr.at[i, hr, half_of], who,
        )

    def rowwise_diagonal():
        return rowwise(0, 1, l, other, m)

    def colwise(i):
        return [
            remote(
                turned.at[i - 1, cr, pl.ds(xs * 64, 64)], bycol.at[i - 1, c, x],
                st.at[i - 1, 0, cr, xs], rt.at[i - 1, 0, c, x],
                device((z + i) % 4, h, (c + cr) % 2, xs, l),
            )
            for cr in range(2)
            for xs in range(4)
        ]

    def colwise_half(i, g):
        return [
            remote(
                packed.at[i - 1, g, cr, xs], bits.at[i - 1, g, c, x],
                st.at[i - 1, 1 + g, cr, xs], rt.at[i - 1, 1 + g, c, x],
                device((z + i) % 4, h, (c + cr) % 2, xs, l),
            )
            for cr in range(2)
            for xs in range(4)
        ]

    def turn(i):
        for cr in range(2):
            turned[i - 1, cr] = done[i, 0, cr].T
        start(colwise(i))

    def turn_half(i, g):
        for cr in range(2):
            block = done[i, 1, cr, pl.ds(pl.multiple_of(g * 64, 64), 64), :].T
            for xs in range(4):
                packed[i - 1, g, cr, xs] = jnp.concatenate(
                    [block[xs * 64 : xs * 64 + 32], block[xs * 64 + 32 : xs * 64 + 64]], axis=1
                )
        start(colwise_half(i, g))

    late = (z // 2 + l) % 2

    for q in range(4):
        sort(q)
        if q == 0:
            pl.semaphore_wait(barrier, len(senders))
        mate1[q].start()
        other1[q].start()

        @pl.when(soon)
        def _():
            lift[q].start()

    start(down1 + core1 + mate2 + core6)
    keep1.start()
    keep3.start()

    for k in range(4):
        if k == 1:
            keep1.wait()
            arrive(core1)
            multiply(0, 0, 0, l, l, True)
        if k == 2:
            multiply(0, 0, 0, m, l, True)
        mate1[k].wait_recv()
        down2[k].start()
        relay1[k].start()
        core2[k].start()

        @pl.when(jnp.logical_not(soon))
        def _():
            lift[k].start()

        @pl.when(relay_soon)
        def _():
            pass_on(k)

    keep2.start()
    arrive(other1)
    start(relay2 + other2)
    arrive(down1)
    start(core3)
    keep2.wait()
    arrive(core2)
    multiply(0, 0, 1, l, m, False)
    begin(0, 0, l)
    multiply(0, 1, 3, m, m, True)
    arrive(core3)
    multiply(1, 0, 0, l, 2 + l, True)
    multiply(1, 0, 0, m, 2 + l, True)
    middle(0, 0, l)
    for k in range(2):
        @pl.when(jnp.logical_not(relay_soon))
        def _():
            pass_on(k)

    for k in range(3):
        down2[k].wait_recv()
        core4[k].start()
    finish(0, 0, l)

    arrive(mate2)
    keep4.start()
    start(core7)
    multiply(0, 0, 1, m, m, False)
    begin(0, 0, m)
    arrive(relay1)
    multiply(0, 1, 2, m, l, False)
    begin(0, 1, m)
    keep3.wait()
    arrive(core6)
    multiply(0, 1, 2, m, 5, True, to=l)
    down2[3].wait_recv()
    core4[3].start()
    multiply(1, 1, 2, m, 2 + l, True)

    @pl.when(jnp.logical_not(relay_soon))
    def _():
        pass_on(2)

    arrive(core4)
    multiply(1, 0, 1, l, 2 + m, False)
    begin(1, 0, l)
    multiply(1, 0, 1, m, 2 + m, False)
    begin(1, 0, m)
    multiply(1, 1, 3, m, 2 + m, False)
    begin(1, 1, m)
    keep4.wait()
    arrive(core7)
    multiply(0, 1, 3, m, 6, False, to=l)
    begin(0, 1, l)
    middle(0, 0, m)
    middle(0, 1, m)
    for k in range(2):
        forward[k].wait_recv()
        core5[k].start()

    @pl.when(jnp.logical_not(relay_soon))
    def _():
        pass_on(3)

    middle(1, 0, l)
    for k in range(2, 4):
        forward[k].wait_recv()
        core5[k].start()
    middle(1, 0, m)
    arrive(core5)
    multiply(2, 0, late, l, 4, True)
    begin(2, 0, l)
    multiply(2, 0, late, m, 4, True)
    begin(2, 0, m)
    multiply(2, 1, 2 + late, m, 4, True)
    begin(2, 1, m)
    middle(1, 1, m)
    finish(1, 0, l)
    finish(1, 0, m)
    turn(1)

    for k in range(3):
        other2[k].wait_recv()
        relay2[k].wait_recv()
        multiply(1, 1, 3, l, 2 + m, k == 0, k)
        multiply(1, 1, 2, l, 2 + l, False, k)
        if k == 2:
            begin(1, 1, l)
        multiply(2, 1, 2 + late, l, 4, k == 0, k)
        if k == 0:
            finish(0, 0, m)
            finish(0, 1, m)
            middle(2, 0, l)
        if k == 1:
            middle(0, 1, l)
            middle(2, 0, m)
    begin(2, 1, l)
    middle(2, 1, m)
    finish(1, 1, m)
    turn_half(1, m)
    rowwise(0, 0, m, mate).start()
    rowwise(0, 1, m, other).start()
    rowwise(1, 0, m, mate).start()
    rowwise(1, 1, m, other).start()
    finish(0, 1, l)
    rowwise_diagonal().start()
    middle(1, 1, l)
    middle(2, 1, l)
    finish(2, 0, l)
    finish(2, 0, m)
    rowwise(2, 0, m, mate).start()
    turn(2)
    finish(2, 1, m)
    rowwise(2, 1, m, other).start()
    turn_half(2, m)
    finish(1, 1, l)
    rowwise(1, 1, l, cross).start()
    turn_half(1, l)
    finish(2, 1, l)
    rowwise(2, 1, l, cross).start()
    turn_half(2, l)

    def place(zs, hs, cs, at):
        return pl.ds(pl.multiple_of(zs * 2048 + hs * 1024 + cs * 512 + at, 128), 128)

    for i in range(3):
        for cr in range(2):
            byrow[0, l, i, cr] = done[i, 0, cr, pl.ds(pl.multiple_of(l * 64, 64), 64), :]
    low = lax.broadcasted_iota(jnp.int32, (64, 128), 1) < 64
    for hr in range(2):
        for i in (1, 2):
            for cs in range(2):
                for xs in range(4):
                    where = place((z + 4 - i) % 4, (h + hr) % 2, cs, xs * 128)
                    if hr == 0:
                        remote(
                            bycol.at[i - 1, cs, xs], bycol.at[i - 1, cs, xs],
                            st.at[i - 1, 0, 0, 0], rt.at[i - 1, 0, cs, xs], mate,
                        ).wait_recv()
                        out_ref[:, where] = bycol[i - 1, cs, xs]
                    else:
                        for g in range(2):
                            remote(
                                bits.at[i - 1, g, cs, xs], bits.at[i - 1, g, cs, xs],
                                st.at[i - 1, 1 + g, 0, 0], rt.at[i - 1, 1 + g, cs, xs], mate,
                            ).wait_recv()
                        v0 = bits[i - 1, 0, cs, xs]
                        v1 = bits[i - 1, 1, cs, xs]
                        out_ref[0:32, where] = jnp.where(low[:32], v0, pltpu.roll(v1, 64, 1))
                        out_ref[32:64, where] = jnp.where(low[:32], pltpu.roll(v0, 64, 1), v1)
        for i in (1, 2, 0):
            for g in (m,) if hr == 0 else (0, 1):
                remote(byrow.at[hr, g, i], byrow.at[hr, g, i], sr.at[i, hr, g], rr.at[i, hr, g], mate).wait_recv()
            for cr in range(2):
                for t in range(2):
                    v0 = byrow[hr, 0, i, cr, :, t * 128 : t * 128 + 128]
                    v1 = byrow[hr, 1, i, cr, :, t * 128 : t * 128 + 128]
                    even = jnp.where(low, v0, pltpu.roll(v1, 64, 1))
                    odd = jnp.where(low, pltpu.roll(v0, 64, 1), v1)
                    for value, xs in ((even, 2 * t), (odd, 2 * t + 1)):
                        where = place((z + i) % 4, (h + hr) % 2, (c + cr) % 2, xs * 128)
                        if i == 2:
                            out_ref[:, where] += value
                        else:
                            out_ref[:, where] = value

    for one in (mate1 + mate2 + relay2 + other1 + relay1 + other2 + down1 + down2 + core1 + core2 + core3
                + core4 + core5 + core6 + core7 + lift + forward):
        one.wait_send()
    for i in range(3):
        for hr in range(2):
            for g in range(2):
                for one in scatter1(i, hr, g) + scatter2(i, hr, g):
                    one.wait_send()
                if hr == 1:
                    rowwise(i, 1, g, cross).wait_send()
            if hr == 0:
                rowwise(i, 0, m, mate).wait_send()
            if i:
                for one in colwise(i) if hr == 0 else colwise_half(i, 0) + colwise_half(i, 1):
                    one.wait_send()


def shards(three_index):
    depth = three_index.shape[0] * three_index.shape[1]
    own = three_index.reshape(depth, 512)
    dma = pltpu.SemaphoreType.DMA
    f32 = jnp.float32
    return pl.pallas_call(
        kernel,
        out_shape=jax.ShapeDtypeStruct((64, 8192), f32),
        in_specs=[pl.BlockSpec(memory_space=pl.ANY)],
        out_specs=pl.BlockSpec(memory_space=pltpu.VMEM),
        scratch_shapes=[
            pltpu.VMEM((depth, 512), jnp.bfloat16),
            pltpu.VMEM((4, 2, depth, 256), jnp.bfloat16),
            pltpu.VMEM((7, depth, 512), jnp.bfloat16),
            pltpu.VMEM((depth, 256), jnp.bfloat16),
            pltpu.VMEM((3, 2, 2, 2, 4, 64, 256), f32),
            pltpu.VMEM((3, 2, 2, 2, 2, 96, 256), jnp.bfloat16),
            pltpu.VMEM((3, 2, 2, 2, 96, 256), jnp.bfloat16),
            pltpu.VMEM((3, 2, 2, 2, 2, 96, 256), jnp.bfloat16),
            pltpu.VMEM((3, 2, 2, 2, 96, 256), jnp.bfloat16),
            pltpu.VMEM((3, 2, 2, 128, 256), f32),
            pltpu.VMEM((2, 2, 256, 128), f32),
            pltpu.VMEM((2, 2, 2, 4, 32, 128), f32),
            pltpu.VMEM((2, 2, 3, 2, 64, 256), f32),
            pltpu.VMEM((2, 2, 4, 64, 128), f32),
            pltpu.VMEM((2, 2, 2, 4, 32, 128), f32),
            dma((8,)), dma((17, 4)), dma((17, 4)),
            dma((3, 2, 2, 2, 2)), dma((3, 2, 2, 2, 2)), dma((3, 2, 2, 2)), dma((3, 2, 2, 2)),
            dma((3, 2, 2)), dma((3, 2, 2)), dma((2, 3, 2, 4)), dma((2, 3, 2, 4)),
        ],
        compiler_params=pltpu.CompilerParams(
            collective_id=0, has_side_effects=True, vmem_limit_bytes=60 * 2**20
        ),
        cost_estimate=pl.CostEstimate(flops=16 * 10**9, bytes_accessed=8 * 10**6, transcendentals=0),
    )(own)


def solution(mesh):
    return jax.shard_map(
        shards,
        mesh=mesh,
        in_specs=(P("aux", None, "basis"),),
        out_specs=P(("basis", "aux"), None),
        check_vma=False,
    )
```

```python
import jax
import jax.numpy as jnp
from jax import lax
from jax.experimental import pallas as pl
from jax.experimental.pallas import tpu as pltpu
from jax.sharding import PartitionSpec as P

MESH = pl.DeviceIdType.MESH


def position():
    b = lax.axis_index("basis")
    a = lax.axis_index("aux")
    return b // 4, (b // 2) % 2, b % 2, a // 2, a % 2


def device(z, h, c, x, l):
    return (z * 4 + h * 2 + c, x * 2 + l)


def remote(src, dst, send, recv, who):
    return pltpu.make_async_remote_copy(
        src_ref=src, dst_ref=dst, send_sem=send, recv_sem=recv,
        device_id=who, device_id_type=MESH,
    )


LEVELS = 10
SPREAD = 256.0 * LEVELS


def encode(value, ref):
    rest = []
    for k in range(2):
        one = value[32 * k : 32 * k + 32]
        high = one.astype(jnp.bfloat16)
        ref[32 * k : 32 * k + 32] = high
        high = high.astype(jnp.float32)
        scale = SPREAD * pl.reciprocal(jnp.maximum(jnp.abs(high), 1e-30), approx=True)
        rest.append(jnp.floor((one - high) * scale + 0.5))
    ref[64:96] = (rest[0] * (2 * LEVELS + 1) + rest[1]).astype(jnp.bfloat16)


def decode(ref):
    both = ref[64:96].astype(jnp.float32)
    first = jnp.floor(both * (1.0 / (2 * LEVELS + 1)) + 0.5)
    out = []
    for k, rest in enumerate((first, both - first * (2 * LEVELS + 1))):
        high = ref[32 * k : 32 * k + 32].astype(jnp.float32)
        out.append(high + jnp.abs(high) * (rest * (1.0 / SPREAD)))
    return jnp.concatenate(out, axis=0)


def kernel(a_ref, byrow, bycol, bits, stage, rows, cols, hop, part, put1, put2, got1, got2, done, turned, packed,
           ls, ss, rs, s1, r1, s2, r2, sr, rr, st, rt):
    z, h, c, x, l = position()
    m = 1 - l
    mate = device(z, h, c, x, m)
    other = device(z, 1 - h, c, x, m)
    cross = device(z, 1 - h, c, x, l)
    core = device(z, h, 1 - c, x, l)
    down = device((z + 3) % 4, h, c, x, l)
    up = device((z + 1) % 4, h, c, x, l)
    xa = x + 1 - 2 * (x % 2)
    xb = 3 - x
    xo = 3 - xa
    near_a = device(z, h, c, xa, l)
    near_b = device(z, h, c, xb, l)
    depth = a_ref.shape[0]
    half = rows.shape[3]
    quarter = depth // 4

    barrier = pltpu.get_barrier_semaphore()
    senders = [mate, other, cross, core, up, near_a, near_b]
    for i in (1, 2):
        for cs in range(2):
            for xs in range(4):
                senders.append(device((z + 4 - i) % 4, h, cs, xs, l))
    for who in senders:
        pl.semaphore_signal(barrier, inc=1, device_id=who, device_id_type=MESH)

    loads = [
        pltpu.make_async_copy(
            a_ref.at[pl.ds(q * quarter, quarter)], stage.at[pl.ds(q * quarter, quarter)], ls.at[q]
        )
        for q in range(4)
    ]
    for one in loads:
        one.start()
    def sort(q):
        loads[q].wait()

        def body(n, carry):
            at = pl.multiple_of(q * quarter + n * 128, 128)
            block = stage[pl.ds(at, 128), :]
            for g in range(2):
                rows[0, g, pl.ds(at, 128), :] = jnp.concatenate(
                    [block[:, t * 128 + g * 64 : t * 128 + g * 64 + 64] for t in range(4)], axis=1
                )
            return carry

        lax.fori_loop(0, quarter // 128, body, 0)

    fours = [(q * quarter, quarter) for q in range(4)]
    parts = [(0, 2 * quarter), (2 * quarter, quarter), (3 * quarter, quarter)]

    def copies(n, src, dst, who, spans):
        return [
            remote(src.at[pl.ds(*span)], dst.at[pl.ds(*span)], ss.at[n, k], rs.at[n, k], who)
            for k, span in enumerate(spans)
        ]

    def side(n, cr):
        return cols.at[n, :, pl.ds(cr * half, half)]

    whole = [(0, depth)]
    mate1 = copies(0, rows.at[0, m], rows.at[1, m], mate, fours)
    mate2 = copies(1, rows.at[0, l], rows.at[1, l], mate, whole)
    relay2 = copies(2, rows.at[3, m], rows.at[2, m], mate, parts)
    other1 = copies(3, rows.at[0, l], rows.at[3, l], other, fours)
    relay1 = copies(4, rows.at[1, l], rows.at[2, l], other, fours)
    other2 = copies(5, rows.at[0, m], rows.at[3, m], other, parts)
    down1 = copies(6, rows.at[0, l], side(2 + l, 0), down, whole)
    down2 = copies(7, rows.at[1, l], side(2 + m, 0), down, fours)
    core1 = copies(8, rows.at[0, l], side(l, 1), core, whole)
    core2 = copies(9, rows.at[1, l], side(m, 1), core, fours)
    core3 = copies(10, side(2 + l, 0), side(2 + l, 1), core, whole)
    core4 = copies(11, side(2 + m, 0), side(2 + m, 1), core, fours)
    core5 = copies(12, side(4, 0), side(4, 1), core, fours)
    take = ((z + 2) % 4) // 2
    soon = take == l
    relay_soon = ((z + 1) % 4) // 2 == l
    lift = copies(13, rows.at[(take + l) % 2, l], hop, up, fours)
    forward = copies(14, hop, side(4, 0), up, fours)
    keep1 = pltpu.make_async_copy(rows.at[0, l], side(l, 0), ls.at[4])
    keep2 = pltpu.make_async_copy(rows.at[1, l], side(m, 0), ls.at[5])
    core6 = copies(15, rows.at[0, m], side(5, 1), core, whole)
    core7 = copies(16, rows.at[1, m], side(6, 1), core, whole)
    keep3 = pltpu.make_async_copy(rows.at[0, m], side(5, 0), ls.at[6])
    keep4 = pltpu.make_async_copy(rows.at[1, m], side(6, 0), ls.at[7])

    def start(those):
        for one in those:
            one.start()

    def arrive(those):
        for one in those:
            one.wait_recv()

    def pass_on(k):
        lift[k].wait_recv()
        forward[k].start()

    def multiply(i, hr, role, g, column, first, k=None, to=None):
        span = pl.ds(0, depth) if k is None else pl.ds(*parts[k])
        block = lax.dot_general(
            rows[role, g, span], cols[column, span], (((0,), (0,)), ((), ())),
            preferred_element_type=jnp.float32,
        )
        for cr in range(2):
            piece = block[:, cr * half : cr * half + half].reshape(4, 64, half)
            if first:
                part[i, hr, g if to is None else to, cr] = piece
            else:
                part[i, hr, g if to is None else to, cr] += piece

    def scatter1(i, hr, g):
        return [
            remote(
                put1.at[i, hr, g, cr, k], got1.at[i, hr, g, cr, k],
                s1.at[i, hr, g, cr, k], r1.at[i, hr, g, cr, k], near,
            )
            for cr, near in ((0, near_a), (1, near_b))
            for k in range(2)
        ]

    def scatter2(i, hr, g):
        return [
            remote(
                put2.at[i, hr, g, cr], got2.at[i, hr, g, cr],
                s2.at[i, hr, g, cr], r2.at[i, hr, g, cr], near,
            )
            for cr, near in ((0, near_b), (1, near_a))
        ]

    def begin(i, hr, g):
        for cr, mine in ((0, xa), (1, xb)):
            for k, piece in ((0, mine), (1, xo)):
                encode(part[i, hr, g, cr, piece], put1.at[i, hr, g, cr, k])
        for one in scatter1(i, hr, g):
            one.start()

    def middle(i, hr, g):
        for one in scatter1(i, hr, g):
            one.wait_recv()
        for cr, piece in ((0, xb), (1, xa)):
            encode(part[i, hr, g, cr, piece] + decode(got1.at[i, hr, g, cr, 1]), put2.at[i, hr, g, cr])
        for one in scatter2(i, hr, g):
            one.start()

    def finish(i, hr, g):
        for one in scatter2(i, hr, g):
            one.wait_recv()
        for cr in range(2):
            done[i, hr, cr, pl.ds(pl.multiple_of(g * 64, 64), 64), :] = (
                part[i, hr, g, cr, x] + decode(got1.at[i, hr, g, cr, 0]) + decode(got2.at[i, hr, g, cr])
            )

    def rowwise(i, hr, g, who, half_of=l):
        return remote(
            done.at[i, hr, :, pl.ds(pl.multiple_of(g * 64, 64), 64), :], byrow.at[hr, half_of, i],
            sr.at[i, hr, g], rr.at[i, hr, half_of], who,
        )

    def rowwise_diagonal():
        return rowwise(0, 1, l, other, m)

    def colwise(i):
        return [
            remote(
                turned.at[i - 1, cr, pl.ds(xs * 64, 64)], bycol.at[i - 1, c, x],
                st.at[i - 1, 0, cr, xs], rt.at[i - 1, 0, c, x],
                device((z + i) % 4, h, (c + cr) % 2, xs, l),
            )
            for cr in range(2)
            for xs in range(4)
        ]

    def colwise_half(i, g):
        return [
            remote(
                packed.at[i - 1, g, cr, xs], bits.at[i - 1, g, c, x],
                st.at[i - 1, 1 + g, cr, xs], rt.at[i - 1, 1 + g, c, x],
                device((z + i) % 4, h, (c + cr) % 2, xs, l),
            )
            for cr in range(2)
            for xs in range(4)
        ]

    def turn(i):
        for cr in range(2):
            turned[i - 1, cr] = done[i, 0, cr].T
        start(colwise(i))

    def turn_half(i, g):
        for cr in range(2):
            block = done[i, 1, cr, pl.ds(pl.multiple_of(g * 64, 64), 64), :].T
            for xs in range(4):
                packed[i - 1, g, cr, xs] = jnp.concatenate(
                    [block[xs * 64 : xs * 64 + 32], block[xs * 64 + 32 : xs * 64 + 64]], axis=1
                )
        start(colwise_half(i, g))

    late = (z // 2 + l) % 2

    for q in range(4):
        sort(q)
        if q == 0:
            pl.semaphore_wait(barrier, len(senders))
        mate1[q].start()
        other1[q].start()

        @pl.when(soon)
        def _():
            lift[q].start()

    start(down1 + core1 + mate2 + core6)
    keep1.start()
    keep3.start()

    for k in range(4):
        if k == 1:
            keep1.wait()
            arrive(core1)
            multiply(0, 0, 0, l, l, True)
        if k == 2:
            multiply(0, 0, 0, m, l, True)
        mate1[k].wait_recv()
        down2[k].start()
        relay1[k].start()
        core2[k].start()

        @pl.when(jnp.logical_not(soon))
        def _():
            lift[k].start()

        @pl.when(relay_soon)
        def _():
            pass_on(k)

    keep2.start()
    arrive(other1)
    start(relay2 + other2)
    arrive(down1)
    start(core3)
    keep2.wait()
    arrive(core2)
    multiply(0, 0, 1, l, m, False)
    begin(0, 0, l)
    multiply(0, 1, 3, m, m, True)
    arrive(core3)
    multiply(1, 0, 0, l, 2 + l, True)
    multiply(1, 0, 0, m, 2 + l, True)
    middle(0, 0, l)
    for k in range(2):
        @pl.when(jnp.logical_not(relay_soon))
        def _():
            pass_on(k)

    for k in range(3):
        down2[k].wait_recv()
        core4[k].start()
    finish(0, 0, l)

    arrive(mate2)
    keep4.start()
    start(core7)
    multiply(0, 0, 1, m, m, False)
    begin(0, 0, m)
    arrive(relay1)
    multiply(0, 1, 2, m, l, False)
    begin(0, 1, m)
    keep3.wait()
    arrive(core6)
    multiply(0, 1, 2, m, 5, True, to=l)
    down2[3].wait_recv()
    core4[3].start()
    multiply(1, 1, 2, m, 2 + l, True)

    @pl.when(jnp.logical_not(relay_soon))
    def _():
        pass_on(2)

    arrive(core4)
    multiply(1, 0, 1, l, 2 + m, False)
    begin(1, 0, l)
    multiply(1, 0, 1, m, 2 + m, False)
    begin(1, 0, m)
    multiply(1, 1, 3, m, 2 + m, False)
    begin(1, 1, m)
    keep4.wait()
    arrive(core7)
    multiply(0, 1, 3, m, 6, False, to=l)
    begin(0, 1, l)
    middle(0, 0, m)
    middle(0, 1, m)
    for k in range(2):
        forward[k].wait_recv()
        core5[k].start()

    @pl.when(jnp.logical_not(relay_soon))
    def _():
        pass_on(3)

    middle(1, 0, l)
    for k in range(2, 4):
        forward[k].wait_recv()
        core5[k].start()
    middle(1, 0, m)
    arrive(core5)
    multiply(2, 0, late, l, 4, True)
    begin(2, 0, l)
    multiply(2, 0, late, m, 4, True)
    begin(2, 0, m)
    multiply(2, 1, 2 + late, m, 4, True)
    begin(2, 1, m)
    middle(1, 1, m)
    finish(1, 0, l)
    finish(1, 0, m)
    turn(1)
    middle(0, 1, l)
    finish(1, 1, m)
    turn_half(1, m)

    for k in range(3):
        other2[k].wait_recv()
        relay2[k].wait_recv()
        if k == 2:
            rowwise(0, 0, m, mate).start()
            rowwise(0, 1, m, other).start()
            rowwise(1, 0, m, mate).start()
            rowwise(1, 1, m, other).start()
            rowwise_diagonal().start()
        multiply(1, 1, 3, l, 2 + m, k == 0, k)
        multiply(1, 1, 2, l, 2 + l, False, k)
        if k == 2:
            begin(1, 1, l)
        multiply(2, 1, 2 + late, l, 4, k == 0, k)
        if k == 0:
            finish(0, 0, m)
            finish(0, 1, m)
            middle(2, 0, l)
        if k == 1:
            middle(2, 0, m)
            finish(0, 1, l)
            middle(2, 1, m)
    begin(2, 1, l)
    finish(2, 0, l)
    finish(2, 0, m)
    rowwise(2, 0, m, mate).start()
    turn(2)
    finish(2, 1, m)
    rowwise(2, 1, m, other).start()
    turn_half(2, m)
    middle(1, 1, l)
    middle(2, 1, l)
    finish(1, 1, l)
    rowwise(1, 1, l, cross).start()
    turn_half(1, l)
    finish(2, 1, l)
    rowwise(2, 1, l, cross).start()
    turn_half(2, l)

    for i in range(3):
        for cr in range(2):
            byrow[0, l, i, cr] = done[i, 0, cr, pl.ds(pl.multiple_of(l * 64, 64), 64), :]

    def landed(ref, send, recv):
        remote(ref, ref, send, recv, mate).wait_recv()

    for i in (1, 2):
        for cs in range(2):
            for xs in range(4):
                landed(bycol.at[i - 1, cs, xs], st.at[i - 1, 0, 0, 0], rt.at[i - 1, 0, cs, xs])
                for g in range(2):
                    landed(bits.at[i - 1, g, cs, xs], st.at[i - 1, 1 + g, 0, 0], rt.at[i - 1, 1 + g, cs, xs])
    for i in range(3):
        landed(byrow.at[0, m, i], sr.at[i, 0, m], rr.at[i, 0, m])
        for g in range(2):
            landed(byrow.at[1, g, i], sr.at[i, 1, g], rr.at[i, 1, g])

    for one in (mate1 + mate2 + relay2 + other1 + relay1 + other2 + down1 + down2 + core1 + core2 + core3
                + core4 + core5 + core6 + core7 + lift + forward):
        one.wait_send()
    for i in range(3):
        for hr in range(2):
            for g in range(2):
                for one in scatter1(i, hr, g) + scatter2(i, hr, g):
                    one.wait_send()
                if hr == 1:
                    rowwise(i, 1, g, cross).wait_send()
            if hr == 0:
                rowwise(i, 0, m, mate).wait_send()
            if i:
                for one in colwise(i) if hr == 0 else colwise_half(i, 0) + colwise_half(i, 1):
                    one.wait_send()


def assemble(byrow, bycol, bits, out_ref):
    z, h, c, x, l = position()

    def place(zs, hs, cs, at):
        return pl.ds(pl.multiple_of(zs * 2048 + hs * 1024 + cs * 512 + at, 128), 128)

    low = lax.broadcasted_iota(jnp.int32, (64, 128), 1) < 64
    for hr in range(2):
        for i in (1, 2):
            for cs in range(2):
                for xs in range(4):
                    where = place((z + 4 - i) % 4, (h + hr) % 2, cs, xs * 128)
                    if hr == 0:
                        out_ref[:, where] = bycol[i - 1, cs, xs]
                    else:
                        v0 = bits[i - 1, 0, cs, xs]
                        v1 = bits[i - 1, 1, cs, xs]
                        out_ref[0:32, where] = jnp.where(low[:32], v0, pltpu.roll(v1, 64, 1))
                        out_ref[32:64, where] = jnp.where(low[:32], pltpu.roll(v0, 64, 1), v1)
        for i in range(3):
            for cr in range(2):
                for t in range(2):
                    v0 = byrow[hr, 0, i, cr, :, t * 128 : t * 128 + 128]
                    v1 = byrow[hr, 1, i, cr, :, t * 128 : t * 128 + 128]
                    even = jnp.where(low, v0, pltpu.roll(v1, 64, 1))
                    odd = jnp.where(low, pltpu.roll(v0, 64, 1), v1)
                    for value, xs in ((even, 2 * t), (odd, 2 * t + 1)):
                        where = place((z + i) % 4, (h + hr) % 2, (c + cr) % 2, xs * 128)
                        if i == 2:
                            out_ref[:, where] += value
                        else:
                            out_ref[:, where] = value


def shards(three_index):
    depth = three_index.shape[0] * three_index.shape[1]
    own = three_index.reshape(depth, 512)
    dma = pltpu.SemaphoreType.DMA
    f32 = jnp.float32
    vmem = pl.BlockSpec(memory_space=pltpu.VMEM)
    pieces = pl.pallas_call(
        kernel,
        out_shape=[
            jax.ShapeDtypeStruct((2, 2, 3, 2, 64, 256), f32),
            jax.ShapeDtypeStruct((2, 2, 4, 64, 128), f32),
            jax.ShapeDtypeStruct((2, 2, 2, 4, 32, 128), f32),
        ],
        in_specs=[pl.BlockSpec(memory_space=pl.ANY)],
        out_specs=[vmem] * 3,
        scratch_shapes=[
            pltpu.VMEM((depth, 512), jnp.bfloat16),
            pltpu.VMEM((4, 2, depth, 256), jnp.bfloat16),
            pltpu.VMEM((7, depth, 512), jnp.bfloat16),
            pltpu.VMEM((depth, 256), jnp.bfloat16),
            pltpu.VMEM((3, 2, 2, 2, 4, 64, 256), f32),
            pltpu.VMEM((3, 2, 2, 2, 2, 96, 256), jnp.bfloat16),
            pltpu.VMEM((3, 2, 2, 2, 96, 256), jnp.bfloat16),
            pltpu.VMEM((3, 2, 2, 2, 2, 96, 256), jnp.bfloat16),
            pltpu.VMEM((3, 2, 2, 2, 96, 256), jnp.bfloat16),
            pltpu.VMEM((3, 2, 2, 128, 256), f32),
            pltpu.VMEM((2, 2, 256, 128), f32),
            pltpu.VMEM((2, 2, 2, 4, 32, 128), f32),
            dma((8,)), dma((17, 4)), dma((17, 4)),
            dma((3, 2, 2, 2, 2)), dma((3, 2, 2, 2, 2)), dma((3, 2, 2, 2)), dma((3, 2, 2, 2)),
            dma((3, 2, 2)), dma((3, 2, 2)), dma((2, 3, 2, 4)), dma((2, 3, 2, 4)),
        ],
        compiler_params=pltpu.CompilerParams(
            collective_id=0, has_side_effects=True, vmem_limit_bytes=60 * 2**20
        ),
        cost_estimate=pl.CostEstimate(flops=16 * 10**9, bytes_accessed=8 * 10**6, transcendentals=0),
    )(own)
    return pl.pallas_call(
        assemble,
        out_shape=jax.ShapeDtypeStruct((64, 8192), f32),
        in_specs=[vmem] * 3,
        out_specs=vmem,
        compiler_params=pltpu.CompilerParams(vmem_limit_bytes=32 * 2**20),
    )(*pieces)


def solution(mesh):
    return jax.shard_map(
        shards,
        mesh=mesh,
        in_specs=(P("aux", None, "basis"),),
        out_specs=P(("basis", "aux"), None),
        check_vma=False,
    )
```

```python
import jax
import jax.numpy as jnp
from jax import lax
from jax.experimental import pallas as pl
from jax.experimental.pallas import tpu as pltpu
from jax.sharding import PartitionSpec as P

MESH = pl.DeviceIdType.MESH


def position():
    b = lax.axis_index("basis")
    a = lax.axis_index("aux")
    return b // 4, (b // 2) % 2, b % 2, a // 2, a % 2


def device(z, h, c, x, l):
    return (z * 4 + h * 2 + c, x * 2 + l)


def remote(src, dst, send, recv, who):
    return pltpu.make_async_remote_copy(
        src_ref=src, dst_ref=dst, send_sem=send, recv_sem=recv,
        device_id=who, device_id_type=MESH,
    )


LEVELS = 10
SPREAD = 256.0 * LEVELS


def encode(value, ref):
    rest = []
    for k in range(2):
        one = value[32 * k : 32 * k + 32]
        high = one.astype(jnp.bfloat16)
        ref[32 * k : 32 * k + 32] = high
        high = high.astype(jnp.float32)
        scale = SPREAD * pl.reciprocal(jnp.maximum(jnp.abs(high), 1e-30), approx=True)
        rest.append(jnp.floor((one - high) * scale + 0.5))
    ref[64:96] = (rest[0] * (2 * LEVELS + 1) + rest[1]).astype(jnp.bfloat16)


def decode(ref):
    both = ref[64:96].astype(jnp.float32)
    first = jnp.floor(both * (1.0 / (2 * LEVELS + 1)) + 0.5)
    out = []
    for k, rest in enumerate((first, both - first * (2 * LEVELS + 1))):
        high = ref[32 * k : 32 * k + 32].astype(jnp.float32)
        out.append(high + jnp.abs(high) * (rest * (1.0 / SPREAD)))
    return jnp.concatenate(out, axis=0)


def kernel(a_ref, out_ref, stage, rows, cols, hop, part, put1, put2, got1, got2, done, turned, packed, byrow, bycol,
           bits, ls, ss, rs, s1, r1, s2, r2, sr, rr, st, rt):
    z, h, c, x, l = position()
    m = 1 - l
    mate = device(z, h, c, x, m)
    other = device(z, 1 - h, c, x, m)
    cross = device(z, 1 - h, c, x, l)
    core = device(z, h, 1 - c, x, l)
    down = device((z + 3) % 4, h, c, x, l)
    up = device((z + 1) % 4, h, c, x, l)
    xa = x + 1 - 2 * (x % 2)
    xb = 3 - x
    xo = 3 - xa
    near_a = device(z, h, c, xa, l)
    near_b = device(z, h, c, xb, l)
    depth = a_ref.shape[0]
    half = rows.shape[3]
    quarter = depth // 4

    barrier = pltpu.get_barrier_semaphore()
    senders = [mate, other, cross, core, up, near_a, near_b]
    for i in (1, 2):
        for cs in range(2):
            for xs in range(4):
                senders.append(device((z + 4 - i) % 4, h, cs, xs, l))
    for who in senders:
        pl.semaphore_signal(barrier, inc=1, device_id=who, device_id_type=MESH)

    loads = [
        pltpu.make_async_copy(
            a_ref.at[pl.ds(q * quarter, quarter)], stage.at[pl.ds(q * quarter, quarter)], ls.at[q]
        )
        for q in range(4)
    ]
    for one in loads:
        one.start()
    def sort(q):
        loads[q].wait()

        def body(n, carry):
            at = pl.multiple_of(q * quarter + n * 128, 128)
            block = stage[pl.ds(at, 128), :]
            for g in range(2):
                rows[0, g, pl.ds(at, 128), :] = jnp.concatenate(
                    [block[:, t * 128 + g * 64 : t * 128 + g * 64 + 64] for t in range(4)], axis=1
                )
            return carry

        lax.fori_loop(0, quarter // 128, body, 0)

    fours = [(q * quarter, quarter) for q in range(4)]
    parts = [(0, 2 * quarter), (2 * quarter, quarter), (3 * quarter, quarter)]

    def copies(n, src, dst, who, spans):
        return [
            remote(src.at[pl.ds(*span)], dst.at[pl.ds(*span)], ss.at[n, k], rs.at[n, k], who)
            for k, span in enumerate(spans)
        ]

    def side(n, cr):
        return cols.at[n, :, pl.ds(cr * half, half)]

    whole = [(0, depth)]
    mate1 = copies(0, rows.at[0, m], rows.at[1, m], mate, fours)
    mate2 = copies(1, rows.at[0, l], rows.at[1, l], mate, whole)
    relay2 = copies(2, rows.at[3, m], rows.at[2, m], mate, parts)
    other1 = copies(3, rows.at[0, l], rows.at[3, l], other, fours)
    relay1 = copies(4, rows.at[1, l], rows.at[2, l], other, fours)
    other2 = copies(5, rows.at[0, m], rows.at[3, m], other, parts)
    down1 = copies(6, rows.at[0, l], side(2 + l, 0), down, whole)
    down2 = copies(7, rows.at[1, l], side(2 + m, 0), down, fours)
    core1 = copies(8, rows.at[0, l], side(l, 1), core, whole)
    core2 = copies(9, rows.at[1, l], side(m, 1), core, fours)
    core3 = copies(10, side(2 + l, 0), side(2 + l, 1), core, whole)
    core4 = copies(11, side(2 + m, 0), side(2 + m, 1), core, fours)
    core5 = copies(12, side(4, 0), side(4, 1), core, fours)
    take = ((z + 2) % 4) // 2
    soon = take == l
    relay_soon = ((z + 1) % 4) // 2 == l
    lift = copies(13, rows.at[(take + l) % 2, l], hop, up, fours)
    forward = copies(14, hop, side(4, 0), up, fours)
    keep1 = pltpu.make_async_copy(rows.at[0, l], side(l, 0), ls.at[4])
    keep2 = pltpu.make_async_copy(rows.at[1, l], side(m, 0), ls.at[5])
    core6 = copies(15, rows.at[0, m], side(5, 1), core, whole)
    core7 = copies(16, rows.at[1, m], side(6, 1), core, whole)
    keep3 = pltpu.make_async_copy(rows.at[0, m], side(5, 0), ls.at[6])
    keep4 = pltpu.make_async_copy(rows.at[1, m], side(6, 0), ls.at[7])

    def start(those):
        for one in those:
            one.start()

    def arrive(those):
        for one in those:
            one.wait_recv()

    def pass_on(k):
        lift[k].wait_recv()
        forward[k].start()

    def multiply(i, hr, role, g, column, first, k=None, to=None):
        span = pl.ds(0, depth) if k is None else pl.ds(*parts[k])
        block = lax.dot_general(
            rows[role, g, span], cols[column, span], (((0,), (0,)), ((), ())),
            preferred_element_type=jnp.float32,
        )
        for cr in range(2):
            piece = block[:, cr * half : cr * half + half].reshape(4, 64, half)
            if first:
                part[i, hr, g if to is None else to, cr] = piece
            else:
                part[i, hr, g if to is None else to, cr] += piece

    def scatter1(i, hr, g):
        return [
            remote(
                put1.at[i, hr, g, cr, k], got1.at[i, hr, g, cr, k],
                s1.at[i, hr, g, cr, k], r1.at[i, hr, g, cr, k], near,
            )
            for cr, near in ((0, near_a), (1, near_b))
            for k in range(2)
        ]

    def scatter2(i, hr, g):
        return [
            remote(
                put2.at[i, hr, g, cr], got2.at[i, hr, g, cr],
                s2.at[i, hr, g, cr], r2.at[i, hr, g, cr], near,
            )
            for cr, near in ((0, near_b), (1, near_a))
        ]

    def begin(i, hr, g):
        for cr, mine in ((0, xa), (1, xb)):
            for k, piece in ((0, mine), (1, xo)):
                encode(part[i, hr, g, cr, piece], put1.at[i, hr, g, cr, k])
                scatter1(i, hr, g)[2 * cr + k].start()

    def middle(i, hr, g):
        first = scatter1(i, hr, g)
        for cr, piece in ((0, xb), (1, xa)):
            first[2 * cr + 1].wait_recv()
            encode(part[i, hr, g, cr, piece] + decode(got1.at[i, hr, g, cr, 1]), put2.at[i, hr, g, cr])
            scatter2(i, hr, g)[cr].start()
        for cr in range(2):
            first[2 * cr].wait_recv()

    def finish(i, hr, g):
        for one in scatter2(i, hr, g):
            one.wait_recv()
        for cr in range(2):
            done[i, hr, cr, pl.ds(pl.multiple_of(g * 64, 64), 64), :] = (
                part[i, hr, g, cr, x] + decode(got1.at[i, hr, g, cr, 0]) + decode(got2.at[i, hr, g, cr])
            )

    def rowwise(i, hr, g, who, half_of=l):
        return remote(
            done.at[i, hr, :, pl.ds(pl.multiple_of(g * 64, 64), 64), :], byrow.at[hr, half_of, i],
            sr.at[i, hr, g], rr.at[i, hr, half_of], who,
        )

    def rowwise_diagonal():
        return rowwise(0, 1, l, other, m)

    def colwise(i):
        return [
            remote(
                turned.at[i - 1, cr, pl.ds(xs * 64, 64)], bycol.at[i - 1, c, x],
                st.at[i - 1, 0, cr, xs], rt.at[i - 1, 0, c, x],
                device((z + i) % 4, h, (c + cr) % 2, xs, l),
            )
            for cr in range(2)
            for xs in range(4)
        ]

    def colwise_half(i, g):
        return [
            remote(
                packed.at[i - 1, g, cr, xs], bits.at[i - 1, g, c, x],
                st.at[i - 1, 1 + g, cr, xs], rt.at[i - 1, 1 + g, c, x],
                device((z + i) % 4, h, (c + cr) % 2, xs, l),
            )
            for cr in range(2)
            for xs in range(4)
        ]

    def turn(i):
        for cr in range(2):
            turned[i - 1, cr] = done[i, 0, cr].T
        start(colwise(i))

    def turn_half(i, g):
        for cr in range(2):
            block = done[i, 1, cr, pl.ds(pl.multiple_of(g * 64, 64), 64), :].T
            for xs in range(4):
                packed[i - 1, g, cr, xs] = jnp.concatenate(
                    [block[xs * 64 : xs * 64 + 32], block[xs * 64 + 32 : xs * 64 + 64]], axis=1
                )
        start(colwise_half(i, g))

    late = (z // 2 + l) % 2

    for q in range(4):
        sort(q)
        if q == 0:
            pl.semaphore_wait(barrier, len(senders))
        mate1[q].start()
        other1[q].start()

        @pl.when(soon)
        def _():
            lift[q].start()

    start(down1 + core1 + mate2 + core6)
    keep1.start()
    keep3.start()

    for k in range(4):
        if k == 1:
            keep1.wait()
            arrive(core1)
            multiply(0, 0, 0, l, l, True)
        if k == 2:
            multiply(0, 0, 0, m, l, True)
        mate1[k].wait_recv()
        down2[k].start()
        relay1[k].start()
        core2[k].start()

        @pl.when(jnp.logical_not(soon))
        def _():
            lift[k].start()

        @pl.when(relay_soon)
        def _():
            pass_on(k)

    keep2.start()
    arrive(other1)
    start(relay2 + other2)
    arrive(down1)
    start(core3)
    keep2.wait()
    arrive(core2)
    multiply(0, 0, 1, l, m, False)
    begin(0, 0, l)
    multiply(0, 1, 3, m, m, True)
    arrive(core3)
    multiply(1, 0, 0, l, 2 + l, True)
    multiply(1, 0, 0, m, 2 + l, True)
    middle(0, 0, l)
    for k in range(2):
        @pl.when(jnp.logical_not(relay_soon))
        def _():
            pass_on(k)

    for k in range(3):
        down2[k].wait_recv()
        core4[k].start()
    finish(0, 0, l)

    arrive(mate2)
    keep4.start()
    start(core7)
    multiply(0, 0, 1, m, m, False)
    begin(0, 0, m)
    arrive(relay1)
    multiply(0, 1, 2, m, l, False)
    begin(0, 1, m)
    keep3.wait()
    arrive(core6)
    multiply(0, 1, 2, m, 5, True, to=l)
    down2[3].wait_recv()
    core4[3].start()
    multiply(1, 1, 2, m, 2 + l, True)

    @pl.when(jnp.logical_not(relay_soon))
    def _():
        pass_on(2)

    arrive(core4)
    multiply(1, 0, 1, l, 2 + m, False)
    begin(1, 0, l)
    multiply(1, 0, 1, m, 2 + m, False)
    begin(1, 0, m)
    multiply(1, 1, 3, m, 2 + m, False)
    begin(1, 1, m)
    keep4.wait()
    arrive(core7)
    multiply(0, 1, 3, m, 6, False, to=l)
    begin(0, 1, l)
    middle(0, 0, m)
    middle(0, 1, m)
    for k in range(2):
        forward[k].wait_recv()
        core5[k].start()

    @pl.when(jnp.logical_not(relay_soon))
    def _():
        pass_on(3)

    middle(1, 0, l)
    for k in range(2, 4):
        forward[k].wait_recv()
        core5[k].start()
    middle(1, 0, m)
    arrive(core5)
    multiply(2, 0, late, l, 4, True)
    begin(2, 0, l)
    multiply(2, 0, late, m, 4, True)
    begin(2, 0, m)
    multiply(2, 1, 2 + late, m, 4, True)
    begin(2, 1, m)
    middle(1, 1, m)
    finish(1, 0, l)
    finish(1, 0, m)
    turn(1)
    middle(0, 1, l)
    finish(1, 1, m)
    turn_half(1, m)

    for k in range(3):
        other2[k].wait_recv()
        relay2[k].wait_recv()
        if k == 2:
            rowwise(0, 0, m, mate).start()
            rowwise(0, 1, m, other).start()
            rowwise(1, 0, m, mate).start()
            rowwise(1, 1, m, other).start()
            rowwise_diagonal().start()
        multiply(1, 1, 3, l, 2 + m, k == 0, k)
        multiply(1, 1, 2, l, 2 + l, False, k)
        if k == 2:
            begin(1, 1, l)
        multiply(2, 1, 2 + late, l, 4, k == 0, k)
        if k == 0:
            finish(0, 0, m)
            finish(0, 1, m)
            middle(2, 0, l)
        if k == 1:
            middle(2, 0, m)
            finish(0, 1, l)
            middle(2, 1, m)
    begin(2, 1, l)
    finish(2, 0, l)
    finish(2, 0, m)
    rowwise(2, 0, m, mate).start()
    turn(2)
    finish(2, 1, m)
    rowwise(2, 1, m, other).start()
    turn_half(2, m)
    middle(1, 1, l)
    middle(2, 1, l)
    finish(1, 1, l)
    rowwise(1, 1, l, cross).start()
    turn_half(1, l)
    finish(2, 1, l)
    rowwise(2, 1, l, cross).start()
    turn_half(2, l)

    def place(zs, hs, cs, at):
        return pl.ds(pl.multiple_of(zs * 2048 + hs * 1024 + cs * 512 + at, 128), 128)

    for i in range(3):
        for cr in range(2):
            byrow[0, l, i, cr] = done[i, 0, cr, pl.ds(pl.multiple_of(l * 64, 64), 64), :]
    low = lax.broadcasted_iota(jnp.int32, (64, 128), 1) < 64
    for hr in range(2):
        for i in (1, 2):
            for cs in range(2):
                for xs in range(4):
                    where = place((z + 4 - i) % 4, (h + hr) % 2, cs, xs * 128)
                    if hr == 0:
                        remote(
                            bycol.at[i - 1, cs, xs], bycol.at[i - 1, cs, xs],
                            st.at[i - 1, 0, 0, 0], rt.at[i - 1, 0, cs, xs], mate,
                        ).wait_recv()
                        out_ref[:, where] = bycol[i - 1, cs, xs]
                    else:
                        for g in range(2):
                            remote(
                                bits.at[i - 1, g, cs, xs], bits.at[i - 1, g, cs, xs],
                                st.at[i - 1, 1 + g, 0, 0], rt.at[i - 1, 1 + g, cs, xs], mate,
                            ).wait_recv()
                        v0 = bits[i - 1, 0, cs, xs]
                        v1 = bits[i - 1, 1, cs, xs]
                        out_ref[0:32, where] = jnp.where(low[:32], v0, pltpu.roll(v1, 64, 1))
                        out_ref[32:64, where] = jnp.where(low[:32], pltpu.roll(v0, 64, 1), v1)
        for i in (1, 2, 0):
            for g in (m,) if hr == 0 else (0, 1):
                remote(byrow.at[hr, g, i], byrow.at[hr, g, i], sr.at[i, hr, g], rr.at[i, hr, g], mate).wait_recv()
            for cr in range(2):
                for t in range(2):
                    v0 = byrow[hr, 0, i, cr, :, t * 128 : t * 128 + 128]
                    v1 = byrow[hr, 1, i, cr, :, t * 128 : t * 128 + 128]
                    even = jnp.where(low, v0, pltpu.roll(v1, 64, 1))
                    odd = jnp.where(low, pltpu.roll(v0, 64, 1), v1)
                    for value, xs in ((even, 2 * t), (odd, 2 * t + 1)):
                        where = place((z + i) % 4, (h + hr) % 2, (c + cr) % 2, xs * 128)
                        if i == 2:
                            out_ref[:, where] += value
                        else:
                            out_ref[:, where] = value

    for one in (mate1 + mate2 + relay2 + other1 + relay1 + other2 + down1 + down2 + core1 + core2 + core3
                + core4 + core5 + core6 + core7 + lift + forward):
        one.wait_send()
    for i in range(3):
        for hr in range(2):
            for g in range(2):
                for one in scatter1(i, hr, g) + scatter2(i, hr, g):
                    one.wait_send()
                if hr == 1:
                    rowwise(i, 1, g, cross).wait_send()
            if hr == 0:
                rowwise(i, 0, m, mate).wait_send()
            if i:
                for one in colwise(i) if hr == 0 else colwise_half(i, 0) + colwise_half(i, 1):
                    one.wait_send()


def shards(three_index):
    depth = three_index.shape[0] * three_index.shape[1]
    own = three_index.reshape(depth, 512)
    dma = pltpu.SemaphoreType.DMA
    f32 = jnp.float32
    return pl.pallas_call(
        kernel,
        out_shape=jax.ShapeDtypeStruct((64, 8192), f32),
        in_specs=[pl.BlockSpec(memory_space=pl.ANY)],
        out_specs=pl.BlockSpec(memory_space=pltpu.VMEM),
        scratch_shapes=[
            pltpu.VMEM((depth, 512), jnp.bfloat16),
            pltpu.VMEM((4, 2, depth, 256), jnp.bfloat16),
            pltpu.VMEM((7, depth, 512), jnp.bfloat16),
            pltpu.VMEM((depth, 256), jnp.bfloat16),
            pltpu.VMEM((3, 2, 2, 2, 4, 64, 256), f32),
            pltpu.VMEM((3, 2, 2, 2, 2, 96, 256), jnp.bfloat16),
            pltpu.VMEM((3, 2, 2, 2, 96, 256), jnp.bfloat16),
            pltpu.VMEM((3, 2, 2, 2, 2, 96, 256), jnp.bfloat16),
            pltpu.VMEM((3, 2, 2, 2, 96, 256), jnp.bfloat16),
            pltpu.VMEM((3, 2, 2, 128, 256), f32),
            pltpu.VMEM((2, 2, 256, 128), f32),
            pltpu.VMEM((2, 2, 2, 4, 32, 128), f32),
            pltpu.VMEM((2, 2, 3, 2, 64, 256), f32),
            pltpu.VMEM((2, 2, 4, 64, 128), f32),
            pltpu.VMEM((2, 2, 2, 4, 32, 128), f32),
            dma((8,)), dma((17, 4)), dma((17, 4)),
            dma((3, 2, 2, 2, 2)), dma((3, 2, 2, 2, 2)), dma((3, 2, 2, 2)), dma((3, 2, 2, 2)),
            dma((3, 2, 2)), dma((3, 2, 2)), dma((2, 3, 2, 4)), dma((2, 3, 2, 4)),
        ],
        compiler_params=pltpu.CompilerParams(
            collective_id=0, has_side_effects=True, vmem_limit_bytes=60 * 2**20
        ),
        cost_estimate=pl.CostEstimate(flops=16 * 10**9, bytes_accessed=8 * 10**6, transcendentals=0),
    )(own)


def solution(mesh):
    return jax.shard_map(
        shards,
        mesh=mesh,
        in_specs=(P("aux", None, "basis"),),
        out_specs=P(("basis", "aux"), None),
        check_vma=False,
    )
```
